128 devices in a mesh: expert: 32 (over x, z, core), shard: 4 (over y).
Axes of the slice: x: 4, y: 4, z: 4, core: 2. Of those that a mesh axis runs over, the one named last changes fastest.
Arguments:
- tokens: bfloat16 [6304, 768], P('expert'), may hold values from -6 to 6
- expert_ids: int32 [2, 6304, 2], P(None, 'expert'), may hold values from 0 to 31, all different within a row; in each aligned block of 197 rows (0 to 196, 197 to 393, ..., all dimensions but the last counted through in order) at most 16 rows name the same one
- norm_gain: bfloat16 [2, 2, 768], replicated, may hold values from 0.5 to 1.5
- norm_bias: bfloat16 [2, 2, 768], replicated, may hold values from -2 to 2
- input_weight: bfloat16 [2, 3, 768, 768], P(None, None, None, 'shard'), may hold values from -0.21875 to 0.21875
- input_bias: bfloat16 [2, 2, 768], P(None, None, 'shard'), may hold values from -2 to 2
- output_weight: bfloat16 [2, 768, 768], P(None, 'shard'), may hold values from -0.875 to 0.875
- output_bias: bfloat16 [2, 768], replicated, may hold values from -2 to 2
- router_weight: bfloat16 [2, 768, 32], replicated, may hold values from -0.15625 to 0.15625
- up_weight: bfloat16 [2, 32, 768, 3072], P(None, 'expert', None, 'shard'), may hold values from -0.21875 to 0.21875
- up_bias: bfloat16 [2, 32, 3072], P(None, 'expert', 'shard'), may hold values from -2 to 2
- down_weight: bfloat16 [2, 32, 3072, 768], P(None, 'expert', 'shard'), may hold values from -1.75 to 1.75
- down_bias: bfloat16 [2, 32, 768], P(None, 'expert'), may hold values from -5 to 5
- cotangent: bfloat16 [6304, 768], P('expert'), may hold values from -6 to 6
Outputs:
- block_output: float32 [6304, 768], P('expert')
- grad_tokens: float32 [6304, 768], P('expert')
- grad_norm_gain: float32 [2, 2, 768], replicated
- grad_norm_bias: float32 [2, 2, 768], replicated
- grad_input_weight: float32 [2, 3, 768, 768], P(None, None, None, 'shard')
- grad_input_bias: float32 [2, 2, 768], P(None, None, 'shard')
- grad_output_weight: float32 [2, 768, 768], P(None, 'shard')
- grad_output_bias: float32 [2, 768], replicated
- grad_router: float32 [2, 768, 32], replicated
- grad_up_weight: float32 [2, 32, 768, 3072], P(None, 'expert', None, 'shard')
- grad_up_bias: float32 [2, 32, 3072], P(None, 'expert', 'shard')
- grad_down_weight: float32 [2, 32, 3072, 768], P(None, 'expert', 'shard')
- grad_down_bias: float32 [2, 32, 768], P(None, 'expert')
The draws below stay inside these ranges and needn't reach their ends.
Inputs may be any that keep to these rules, and one draw needn't show every extreme that they name: `expert_ids`: each token names two different experts in each block; within each aligned block of 197 tokens of one block l, no expert is named by more than 16 tokens, a bound that some block reaches; every expert is named somewhere.
All inputs are finite; a program needn't handle non-finite values.
Results may differ from the reference program's by a relative error of at most 0.035.
Values may be sent and summed in bfloat16 or wider, within the bound.
No kernel may reach another device: no remote copies, remote signals or barrier semaphores. Data moves between devices by JAX's collectives and lax.ppermute only.
A program may use at most 128 MiB of HBM per device.

```python
import math
import jax
import jax.numpy as jnp
import numpy as np
from jax import lax

D = 768
HEADS = 12
HEAD = 64
FF = 3072
SEQ = 197
LAYERS = 2
TOK_DEV = 197
TOKENS = 6304
IMAGES = 32
EXPERTS = 32
CAP = 16
N_EXPERT = 32


def block_scale(stream_key, shape, shards, least, high):
    factor_of, own = 1.0, jax.random.fold_in(stream_key, 6)
    for dim, blocks in shards:
        heights = jnp.exp(jax.random.uniform(jax.random.fold_in(own, dim), (blocks,), jnp.float32, least / len(shards), high / len(shards)))
        factor_of = factor_of * jnp.repeat(heights, shape[dim] // blocks).reshape([-1 if axis == dim else 1 for axis in range(len(shape))])
    return factor_of


def assign_block(own_key, own, number, rows, number_of, top, most, skew):
    sequence = jax.random.permutation(own_key, number_of)
    packed, common = portions_of(number_of, rows * top, most, skew, True), portions_of(number_of, rows * top, most, skew, False)
    places = jnp.arange(number_of)

    def named(lengths, offset_by):
        used = int((lengths > 0).sum())
        fixed = max(1, used // 4)
        passed = fixed + (places - fixed + offset_by * (used - fixed)) % max(1, number_of - fixed)
        return jnp.zeros((number_of,), jnp.int32).at[sequence[jnp.where(places < fixed, places, passed)]].set(jnp.asarray(lengths, jnp.int32))

    lengths = jnp.where(number % 4 == 0, named(packed, number // 4), named(common, number - number // 4 - 1))
    mixed = jax.random.permutation(jax.random.fold_in(own, 3), number_of)
    donor, taker = mixed[0:number_of // 2 * 2:2], mixed[1:number_of // 2 * 2:2]
    slack = jnp.minimum(lengths[donor] - 1, most - lengths[taker]) // 2
    slack = jnp.where((donor == sequence[0]) | (taker == sequence[0]) | (lengths[taker] == 0), 0, jnp.maximum(slack, 0))
    passed = jax.random.randint(jax.random.fold_in(own, 4), (number_of // 2,), 0, 1 << 20) % (slack + 1)
    lengths = lengths.at[donor].add(-passed).at[taker].add(passed)
    labels = jnp.searchsorted(jnp.cumsum(lengths), jnp.arange(rows * top), side="right").astype(jnp.int32)
    table = labels.reshape(top, rows).T
    table = table[jax.random.permutation(jax.random.fold_in(own, 1), rows)]
    offset_by = jax.random.randint(jax.random.fold_in(own, 2), (rows, 1), 0, top)
    return jnp.take_along_axis(table, (jnp.arange(top)[None, :] + offset_by) % top, axis=1)


def portions_of(number_of, total, reach, slope, full):
    weights = [(1 << 20) // math.isqrt(standing ** slope) + 1 for standing in range(1, number_of + 1)]
    largest = reach if full else min(reach, max(-(-total // number_of), total * weights[0] // sum(weights)))
    least = 1 if total - largest >= number_of - 1 else 0
    counts, rest = [largest] + [least] * (number_of - 1), total - largest - least * (number_of - 1)
    while rest > 0:
        movable = [i for i in range(1, number_of) if counts[i] < largest] or [i for i in range(1, number_of) if counts[i] < reach]
        pool, budget = sum([weights[i] for i in movable]), rest
        for i in movable:
            addition = min(reach - counts[i], max(1, budget * weights[i] // pool), rest)
            counts[i] = counts[i] + addition
            rest = rest - addition
    return np.array(counts)


def bell_draw(own_key, dims, deviation, most, shards=(), kind=jnp.bfloat16):
    level = block_scale(own_key, dims, shards, -0.22, 0.18) if shards else 1.0
    drawn = jax.random.normal(own_key, dims, jnp.float32) * deviation * level
    return jnp.minimum(jnp.maximum(drawn, -most), most).astype(kind)


def setup_inputs(seed: int = 0) -> dict:
    arg_keys = jax.random.split(jax.random.key(seed), 15)
    tokens = bell_draw(arg_keys[0], (TOKENS, D), 1.0, 6.0, ((0, 32),))
    expert_ids_keys = jax.random.split(jax.random.fold_in(arg_keys[1], 1), LAYERS * TOKENS // TOK_DEV)
    expert_ids_turns = jax.random.permutation(jax.random.fold_in(arg_keys[1], 3), LAYERS * TOKENS // TOK_DEV)
    expert_ids = jax.vmap(lambda own, number: assign_block(jax.random.fold_in(arg_keys[1], 2), own, number, TOK_DEV, EXPERTS, 2, CAP, 1))(expert_ids_keys, expert_ids_turns).reshape((LAYERS, TOKENS, 2))
    norm_gain = jnp.clip(1.0 + 0.1 * jax.random.normal(arg_keys[2], (LAYERS, 2, D), jnp.float32), 0.5, 1.5).astype(jnp.bfloat16)
    norm_bias = bell_draw(arg_keys[3], (LAYERS, 2, D), 0.3, 2.0)
    input_weight = bell_draw(arg_keys[4], (LAYERS, 3, D, D), D ** -0.5, 0.21875, ((3, 4),))
    input_bias = bell_draw(arg_keys[5], (LAYERS, 2, D), 0.3, 2.0, ((2, 4),))
    output_weight = bell_draw(arg_keys[6], (LAYERS, D, D), (D // 16) ** -0.5, 0.875, ((1, 4),))
    output_bias = bell_draw(arg_keys[7], (LAYERS, D), 0.3, 2.0)
    router_weight = bell_draw(arg_keys[8], (LAYERS, D, EXPERTS), (2 * D) ** -0.5, 0.15625)
    up_weight = bell_draw(arg_keys[9], (LAYERS, EXPERTS, D, FF), D ** -0.5, 0.21875, ((1, 32), (3, 4)))
    up_bias = bell_draw(arg_keys[10], (LAYERS, EXPERTS, FF), 0.3, 2.0, ((1, 32), (2, 4)))
    down_weight = bell_draw(arg_keys[11], (LAYERS, EXPERTS, FF, D), (max(FF // 256, 1)) ** -0.5, 1.75, ((1, 32), (2, 4)))
    down_bias = bell_draw(arg_keys[12], (LAYERS, EXPERTS, D), 1.0, 5.0, ((1, 32),))
    cotangent = bell_draw(arg_keys[13], (TOKENS, D), 1.0, 6.0, ((0, 32),))
    return dict(tokens=tokens, expert_ids=expert_ids, norm_gain=norm_gain, norm_bias=norm_bias, input_weight=input_weight, input_bias=input_bias, output_weight=output_weight, output_bias=output_bias, router_weight=router_weight, up_weight=up_weight, up_bias=up_bias, down_weight=down_weight, down_bias=down_bias, cotangent=cotangent)


@jax.custom_vjp
def low(v):
    return lax.optimization_barrier(v.astype(jnp.bfloat16)).astype(jnp.float32)

@jax.custom_vjp
def low_back(v):
    return v

def low_keep(v):
    return (low(v), None)

def low_pass(kept, grad):
    return (grad,)

def back_keep(v):
    return (v, None)

def back_low(kept, grad):
    return (low(grad),)
low.defvjp(low_keep, low_pass)
low_back.defvjp(back_keep, back_low)
eps = 1e-06

def product(form, left, right):
    return jnp.einsum(form, left, right, precision=lax.Precision.HIGHEST)

def layer_norm(values, gain_row, offset):
    centred = values - lax.optimization_barrier(jnp.mean(values, axis=1, keepdims=True))
    inverse = lax.rsqrt(lax.optimization_barrier(jnp.mean(centred * centred, axis=1, keepdims=True)) + eps)
    return centred * inverse * gain_row + offset

def slot_rows(choose):
    blocks = choose.reshape(N_EXPERT, TOK_DEV * 2)
    onehot = (blocks[:, :, None] == jnp.arange(EXPERTS, dtype=jnp.int32)[None, None, :]).astype(jnp.int32)
    placed = lax.optimization_barrier(jnp.sum(jnp.cumsum(onehot, axis=1) * onehot, axis=2)) - 1
    source = jnp.arange(N_EXPERT, dtype=jnp.int32)[:, None]
    return (source * CAP + placed).reshape(TOKENS, 2).astype(jnp.int32)

def forward(tokens, norm_gain, norm_bias, input_weight, input_bias, output_weight, output_bias, router_weight, up_weight, up_bias, down_weight, down_bias, expert_ids):
    hidden = tokens
    score_scale = HEAD ** (-0.5)
    shape_four = (IMAGES, SEQ, HEADS, HEAD)
    for layer_index in range(LAYERS):
        first = low(layer_norm(hidden, norm_gain[layer_index, 0], norm_bias[layer_index, 0]))
        queries = low(low_back(product('td,dc->tc', first, input_weight[layer_index, 0]) + input_bias[layer_index, 0]))
        keys_low = low(low_back(product('td,dc->tc', first, input_weight[layer_index, 1])))
        values_low = low(low_back(product('td,dc->tc', first, input_weight[layer_index, 2]) + input_bias[layer_index, 1]))
        scores = low_back(product('bqhd,bkhd->bhqk', queries.reshape(shape_four), keys_low.reshape(shape_four)) * score_scale)
        weights = low(jax.nn.softmax(scores, axis=3))
        context = product('bhqk,bkhd->bqhd', weights, values_low.reshape(shape_four)).reshape(TOKENS, D)
        context = low(low_back(context))
        middle = hidden + low_back(product('tc,cd->td', context, output_weight[layer_index])) + output_bias[layer_index]
        second = low(layer_norm(middle, norm_gain[layer_index, 1], norm_bias[layer_index, 1]))
        logits = low_back(product('td,de->te', second, router_weight[layer_index]))
        router_prob = jax.nn.softmax(logits, axis=1)
        choose = expert_ids[layer_index]
        gate_values = jnp.take_along_axis(router_prob, choose, axis=1)
        flat_ids = choose.reshape(-1)
        flat_rows = slot_rows(choose).reshape(-1)
        buffer = jnp.zeros((EXPERTS, N_EXPERT * CAP, D), jnp.float32)
        buffer = buffer.at[flat_ids, flat_rows].add(jnp.repeat(second, 2, axis=0))
        buffer = low_back(buffer)
        expert_pre = low_back(product('erd,edf->erf', buffer, up_weight[layer_index]) + up_bias[layer_index][:, None, :])
        active = low(jax.nn.gelu(expert_pre, approximate=False))
        result = product('erf,efd->erd', active, down_weight[layer_index]) + down_bias[layer_index][:, None, :]
        result = low(low_back(result))
        chosen = result[flat_ids, flat_rows].reshape(TOKENS, 2, D)
        hidden = middle + lax.optimization_barrier(jnp.sum(gate_values[:, :, None] * chosen, axis=1))
    return hidden

def reference(tokens, expert_ids, norm_gain, norm_bias, input_weight, input_bias, output_weight, output_bias, router_weight, up_weight, up_bias, down_weight, down_bias, cotangent):
    floats = (tokens.astype(jnp.float32), norm_gain.astype(jnp.float32), norm_bias.astype(jnp.float32), input_weight.astype(jnp.float32), input_bias.astype(jnp.float32), output_weight.astype(jnp.float32), output_bias.astype(jnp.float32), router_weight.astype(jnp.float32), up_weight.astype(jnp.float32), up_bias.astype(jnp.float32), down_weight.astype(jnp.float32), down_bias.astype(jnp.float32))

    def run(tok_in, gain_in, shift_in, inw_in, inb_in, outw_in, outb_in, route_in, upw_in, upb_in, downw_in, downb_in):
        return forward(tok_in, gain_in, shift_in, inw_in, inb_in, outw_in, outb_in, route_in, upw_in, upb_in, downw_in, downb_in, expert_ids)
    output, pullback = jax.vjp(run, floats[0], floats[1], floats[2], floats[3], floats[4], floats[5], floats[6], floats[7], floats[8], floats[9], floats[10], floats[11])
    grads = pullback(cotangent.astype(jnp.float32))
    return (output, grads[0], grads[1], grads[2], grads[3], grads[4], grads[5], grads[6], grads[7], grads[8], grads[9], grads[10], grads[11])
```

```python
import jax
import jax.numpy as jnp
from jax import lax
from jax.experimental import pallas as pl
from jax.experimental.pallas import tpu as pltpu
from jax.sharding import PartitionSpec as P

HEAD = 64
SEQ = 197
BF = jnp.bfloat16
F32 = jnp.float32

eps = 1e-06


def norm_forward(values, gain_row, offset):
    centred = values - jnp.mean(values, axis=1, keepdims=True)
    inverse = lax.rsqrt(jnp.mean(centred * centred, axis=1, keepdims=True) + eps)
    normed = centred * inverse
    return (normed * gain_row + offset, normed, inverse)


def norm_backward(incoming, normed, inverse, gain_row):
    scaled = incoming * gain_row
    return inverse * (
        scaled
        - jnp.mean(scaled, axis=1, keepdims=True)
        - normed * jnp.mean(scaled * normed, axis=1, keepdims=True)
    )


def gelu_slope(values):
    return (
        0.5 * (1.0 + lax.erf(values * 0.7071067811865476))
        + values * jnp.exp(-0.5 * values * values) * 0.3989422804014327
    )


def slot_table(choose, experts, capacity):
    flat_ids = choose.reshape(-1)
    onehot = (flat_ids[:, None] == jnp.arange(experts, dtype=jnp.int32)[None, :]).astype(jnp.int32)
    placed = jnp.sum(jnp.cumsum(onehot, axis=0) * onehot, axis=1) - 1
    column = flat_ids * capacity + placed
    lookup = column[:, None] == jnp.arange(experts * capacity, dtype=jnp.int32)[None, :]
    lookup = lookup.astype(BF).reshape(choose.shape[0], 2, experts * capacity)
    half = capacity // 2
    column = (placed // half) * (experts * half) + flat_ids * half + placed % half
    fetch = column[:, None] == jnp.arange(experts * capacity, dtype=jnp.int32)[None, :]
    return lookup, fetch.astype(BF).reshape(lookup.shape)


def cycle(size, step):
    return [(place, (place + step) % size) for place in range(size)]


def gather_cycle(value, axis, me, size, pairs):
    parts = [value] + [lax.ppermute(value, axis, pairs(step)) for step in range(1, size)]
    stacked = jnp.stack(parts)
    return jnp.stack(
        [
            lax.dynamic_index_in_dim(stacked, (me - place) % size, 0, keepdims=False)
            for place in range(size)
        ]
    )


def sum_cycle(blocks, axis, me, size, pairs):
    total = lax.dynamic_index_in_dim(blocks, me, 0, keepdims=False).astype(F32)
    for step in range(1, size):
        away = lax.dynamic_index_in_dim(blocks, (me + step) % size, 0, keepdims=False)
        total = total + lax.ppermute(away, axis, pairs(step)).astype(F32)
    return total


def dot(left, right):
    return jnp.dot(left, right, preferred_element_type=F32)


def ein(form, left, right):
    return jnp.einsum(form, left, right, preferred_element_type=F32)


def to_owners(buffer, devices):
    outgoing = buffer.reshape(devices, buffer.shape[0] // devices, buffer.shape[1])
    arrived = lax.all_to_all(outgoing, "expert", split_axis=0, concat_axis=0, tiled=True)
    return arrived


def summed_rows(arrived, devices, shards):
    _, half, width = arrived.shape
    total = jnp.sum(arrived.reshape(devices, shards, half, width).astype(F32), axis=1).astype(BF)
    rows = total.reshape(devices * half, width)
    tile, part = width // 3, width // 6
    lower = jnp.concatenate([rows[:, :tile], rows[:, 2 * tile : 2 * tile + part]], axis=1)
    upper = jnp.concatenate([rows[:, tile : 2 * tile], rows[:, 2 * tile + part :]], axis=1)
    return jnp.concatenate([lower, upper], axis=0)


def join_shares(every):
    shares, _, width = every.shape
    tile = 2 * width // 3
    return jnp.concatenate(
        [every[j, :, :tile] for j in range(shares)] + [every[j, :, tile:] for j in range(shares)],
        axis=1,
    ).astype(F32)


def dot_nt(left, right):
    return lax.dot_general(left, right, (((1,), (1,)), ((), ())), preferred_element_type=F32)


def dot_tn(left, right):
    return lax.dot_general(left, right, (((0,), (0,)), ((), ())), preferred_element_type=F32)


def write_chunks(total, out_ref):
    devices, _, half, _ = out_ref.shape
    rows = total.reshape(devices, 2 * half, total.shape[1])
    lower, upper = rows[:, :half], rows[:, half:]
    tile = total.shape[1] // 6
    part = tile // 2
    for j in range(4):
        first = slice(j * tile, (j + 1) * tile)
        rest = slice(4 * tile + j * part, 4 * tile + (j + 1) * part)
        mixed = jnp.concatenate([lower[:, :, rest], upper[:, :, rest]], axis=2)
        block = jnp.concatenate([lower[:, :, first], upper[:, :, first], mixed], axis=2)
        out_ref[:, j] = block.astype(BF)


def forward_kernel(x_ref, up_ref, up_bias_ref, down_ref, offset_ref, chunk_ref, active_ref, slope_ref, total):
    step = pl.program_id(0)
    rows = x_ref[...].reshape(total.shape)
    pre = jnp.dot(rows, up_ref[0, 0], preferred_element_type=F32) + up_bias_ref[0].astype(F32)
    half_cdf = 0.5 * (1.0 + lax.erf(pre * 0.7071067811865476))
    active = (pre * half_cdf).astype(BF)
    active_ref[...] = active
    slope_ref[...] = half_cdf + pre * jnp.exp(-0.5 * pre * pre) * 0.3989422804014327
    part = jnp.dot(active, down_ref[0, 0], preferred_element_type=F32)

    @pl.when(step == 0)
    def _():
        total[...] = part + offset_ref[...]

    @pl.when(step > 0)
    def _():
        total[...] += part

    @pl.when(step == pl.num_programs(0) - 1)
    def _():
        write_chunks(total[...], chunk_ref)


def backward_kernel(dy_ref, slope_ref, up_ref, down_ref, chunk_ref, pre_grad_ref, total):
    step = pl.program_id(0)
    out_grad = dy_ref[...].reshape(total.shape)
    pre_grad = (dot_nt(out_grad, down_ref[0, 0]) * slope_ref[...]).astype(BF)
    pre_grad_ref[...] = pre_grad
    part = dot_nt(pre_grad, up_ref[0, 0])

    @pl.when(step == 0)
    def _():
        total[...] = part

    @pl.when(step > 0)
    def _():
        total[...] += part

    @pl.when(step == pl.num_programs(0) - 1)
    def _():
        write_chunks(total[...], chunk_ref)


def weight_kernel(x_ref, dy_ref, active_ref, pre_grad_ref, *rest):
    up_ref, up_bias_ref, down_ref, down_bias_ref = rest[-4:]
    shape = active_ref.shape[0], x_ref.shape[2]
    pre_grad = pre_grad_ref[...]
    out_grad = dy_ref[...].reshape(shape)
    up_ref[0, 0] = dot_tn(x_ref[...].reshape(shape), pre_grad)
    down_ref[0, 0] = dot_tn(active_ref[...], out_grad)
    up_bias_ref[0] = jnp.sum(pre_grad.astype(F32), axis=0, keepdims=True)

    @pl.when(pl.program_id(0) == 0)
    def _():
        down_bias_ref[0] = jnp.sum(out_grad.astype(F32), axis=0, keepdims=True)


FBLOCK = 256
PARAMS = dict(vmem_limit_bytes=48 * 1024 * 1024)


def whole(shape):
    return pl.BlockSpec(shape, lambda step: (0,) * len(shape))


def expert_forward(layer, arrived, up_weight, up_bias, down_weight, offset):
    devices, slots, width = arrived.shape
    hidden = up_weight.shape[3]
    rows = devices * slots
    return pl.pallas_call(
        forward_kernel,
        grid=(hidden // FBLOCK,),
        in_specs=[
            whole(arrived.shape),
            pl.BlockSpec((1, 1, width, FBLOCK), lambda step: (layer, 0, 0, step)),
            pl.BlockSpec((1, 1, FBLOCK), lambda step: (layer, 0, step)),
            pl.BlockSpec((1, 1, FBLOCK, width), lambda step: (layer, 0, step, 0)),
            whole(offset.shape),
        ],
        out_specs=[
            whole((devices, 4, slots // 2, width // 2)),
            pl.BlockSpec((rows, FBLOCK), lambda step: (0, step)),
            pl.BlockSpec((rows, FBLOCK), lambda step: (0, step)),
        ],
        out_shape=[
            jax.ShapeDtypeStruct((devices, 4, slots // 2, width // 2), BF),
            jax.ShapeDtypeStruct((rows, hidden), BF),
            jax.ShapeDtypeStruct((rows, hidden), F32),
        ],
        scratch_shapes=[pltpu.VMEM((rows, width), F32)],
        compiler_params=pltpu.CompilerParams(**PARAMS),
        name="expert_forward",
    )(arrived, up_weight, up_bias, down_weight, offset)


def expert_backward(layer, out_grad, slope, up_weight, down_weight):
    devices, slots, width = out_grad.shape
    hidden = up_weight.shape[3]
    rows = devices * slots
    return pl.pallas_call(
        backward_kernel,
        grid=(hidden // FBLOCK,),
        in_specs=[
            whole(out_grad.shape),
            pl.BlockSpec((rows, FBLOCK), lambda step: (0, step)),
            pl.BlockSpec((1, 1, width, FBLOCK), lambda step: (layer, 0, 0, step)),
            pl.BlockSpec((1, 1, FBLOCK, width), lambda step: (layer, 0, step, 0)),
        ],
        out_specs=[
            whole((devices, 4, slots // 2, width // 2)),
            pl.BlockSpec((rows, FBLOCK), lambda step: (0, step)),
        ],
        out_shape=[
            jax.ShapeDtypeStruct((devices, 4, slots // 2, width // 2), BF),
            jax.ShapeDtypeStruct((rows, hidden), BF),
        ],
        scratch_shapes=[pltpu.VMEM((rows, width), F32)],
        compiler_params=pltpu.CompilerParams(**PARAMS),
        name="expert_backward",
    )(out_grad, slope, up_weight, down_weight)


def expert_weights(layer, layers, arrived, out_grad, active, pre_grad, earlier):
    devices, slots, width = out_grad.shape
    rows, hidden = active.shape
    operands = [arrived, out_grad, active, pre_grad] + list(earlier or ())
    return pl.pallas_call(
        weight_kernel,
        grid=(hidden // FBLOCK,),
        in_specs=[
            whole(arrived.shape),
            whole(out_grad.shape),
            pl.BlockSpec((rows, FBLOCK), lambda step: (0, step)),
            pl.BlockSpec((rows, FBLOCK), lambda step: (0, step)),
        ]
        + [pl.BlockSpec(memory_space=pl.ANY)] * len(earlier or ()),
        out_specs=[
            pl.BlockSpec((1, 1, width, FBLOCK), lambda step: (layer, 0, 0, step)),
            pl.BlockSpec((1, 1, FBLOCK), lambda step: (layer, 0, step)),
            pl.BlockSpec((1, 1, FBLOCK, width), lambda step: (layer, 0, step, 0)),
            pl.BlockSpec((1, 1, width), lambda step: (layer, 0, 0)),
        ],
        out_shape=[
            jax.ShapeDtypeStruct((layers, 1, width, hidden), F32),
            jax.ShapeDtypeStruct((layers, 1, hidden), F32),
            jax.ShapeDtypeStruct((layers, 1, hidden, width), F32),
            jax.ShapeDtypeStruct((layers, 1, width), F32),
        ],
        input_output_aliases={4 + i: i for i in range(len(earlier or ()))},
        compiler_params=pltpu.CompilerParams(**PARAMS),
        name="expert_weights",
    )(*operands)


def body(
    tokens,
    expert_ids,
    norm_gain,
    norm_bias,
    input_weight,
    input_bias,
    output_weight,
    output_bias,
    router_weight,
    up_weight,
    up_bias,
    down_weight,
    down_bias,
    cotangent,
):
    token_count, width = tokens.shape
    layer_count = norm_gain.shape[0]
    local_width = input_weight.shape[3]
    local_heads = local_width // HEAD
    experts = router_weight.shape[2]
    devices = lax.axis_size("expert")
    shards = lax.axis_size("shard")
    capacity = 5 * token_count // (2 * experts) + 1
    score_scale = HEAD ** (-0.5)
    shape_three = (token_count, local_heads, HEAD)
    expert_range = jnp.arange(experts, dtype=jnp.int32)
    me = lax.axis_index("shard")
    place = lax.axis_index("expert")
    row_block = 8 * (-(-token_count // (8 * shards)))
    rows_padded = row_block * shards

    def shard_pairs(step):
        return cycle(shards, step)

    def gather_shard(value):
        return gather_cycle(value, "shard", me, shards, shard_pairs)

    gathered_out = [gather_shard(output_weight[0])]

    def attention_forward(layer, hidden):
        normed, unit, inverse = norm_forward(
            hidden, norm_gain[layer, 0].astype(F32), norm_bias[layer, 0].astype(F32)
        )
        first_low = normed.astype(BF)
        queries = (
            dot(first_low, input_weight[layer, 0]) + input_bias[layer, 0].astype(F32)
        ).astype(BF)
        keys_low = dot(first_low, input_weight[layer, 1]).astype(BF)
        values_low = (
            dot(first_low, input_weight[layer, 2]) + input_bias[layer, 1].astype(F32)
        ).astype(BF)
        queries, keys_low, values_low = (
            part.reshape(shape_three) for part in (queries, keys_low, values_low)
        )
        scores = ein("qhd,khd->hqk", queries, keys_low) * score_scale
        raised = jnp.exp(scores - jnp.max(scores, axis=2, keepdims=True))
        weights = raised / jnp.sum(raised, axis=2, keepdims=True)
        weights_low = weights.astype(BF)
        context = ein("hqk,khd->qhd", weights_low, values_low)
        context = context.reshape(token_count, local_width).astype(BF)
        everywhere = gather_shard(context)
        head_mix = ein("jtc,jcd->td", everywhere, gathered_out[layer])
        middle = hidden + head_mix + output_bias[layer].astype(F32)
        kept = (first_low, unit, inverse, queries, keys_low, values_low, weights, context)
        return middle, kept

    def route(layer, middle):
        normed, unit, inverse = norm_forward(
            middle, norm_gain[layer, 1].astype(F32), norm_bias[layer, 1].astype(F32)
        )
        second_low = normed.astype(BF)
        logits = dot(second_low, router_weight[layer])
        exps = jnp.exp(logits - jnp.max(logits, axis=1, keepdims=True))
        router_prob = exps / jnp.sum(exps, axis=1, keepdims=True)
        choose = expert_ids[layer]
        picked = (choose[:, :, None] == expert_range[None, None, :]).astype(F32)
        gate_values = jnp.sum(picked * router_prob[:, None, :], axis=2)
        return second_low, unit, inverse, router_prob, picked, gate_values

    def run_forward(layer, arrived):
        offset = jnp.where(me == 0, down_bias[layer].astype(F32), 0.0)
        return expert_forward(layer, arrived, up_weight, up_bias, down_weight, offset)

    def go_back(chunks):
        chunks = chunks.reshape(-1, *chunks.shape[2:])
        return lax.all_to_all(
            chunks, ("expert", "shard"), split_axis=0, concat_axis=0, tiled=True
        )

    def join_columns(value):
        return join_shares(gather_shard(value))

    def slot_grads(lookup, gate_values, incoming):
        slot_grad = (gate_values[:, :, None] * incoming[:, None, :]).astype(BF)
        return ein("tkc,tkd->cd", lookup, slot_grad).astype(BF)

    def own_columns(value):
        tile = 2 * local_width // 3
        first = lax.dynamic_slice_in_dim(value, me * tile, tile, 1)
        rest = lax.dynamic_slice_in_dim(value[:, shards * tile :], me * (tile // 2), tile // 2, 1)
        return jnp.concatenate([first, rest], axis=1)

    def pack_of(second_low, logit_grad, dn2, unit_two, dh2, dz, context, first_low, qkv_grad):
        ones = jnp.ones((token_count, 1), F32)
        zeros = jnp.zeros((width, 1), F32)
        in_rows = jnp.sum(qkv_grad.astype(F32), axis=0).reshape(3, local_width)
        bias_rows = jnp.concatenate([in_rows[0], in_rows[2]])
        bias_column = jnp.pad(bias_rows, (0, width - 2 * local_width))[:, None]
        sums = jnp.stack(
            [jnp.sum(dn2 * unit_two, axis=0), jnp.sum(dn2, axis=0), jnp.sum(dh2, axis=0)], axis=1
        )
        pack = jnp.concatenate(
            [
                ein("td,tc->dc", first_low, qkv_grad),
                ein("td,tc->dc", dz, context),
                ein("td,te->de", second_low, logit_grad),
                sums,
                bias_column,
            ],
            axis=1,
        )
        return pack.astype(BF)

    hidden = tokens.astype(F32)
    stored = []
    for layer in range(layer_count - 1):
        middle, attention_kept = attention_forward(layer, hidden)
        routed = route(layer, middle)
        second_low, gate_values = routed[0], routed[5]
        lookup, fetch = slot_table(expert_ids[layer], experts, capacity)
        dispatch = ein("tc,td->cd", lookup[:, 0] + lookup[:, 1], second_low).astype(BF)
        arrived = to_owners(dispatch, devices)
        arrived, later_weight = lax.optimization_barrier((arrived, output_weight[layer + 1]))
        gathered_out.append(gather_shard(later_weight))
        chunks, active, slope = run_forward(layer, arrived)
        returned = summed_rows(go_back(chunks), devices, shards)
        chosen = ein("tkc,cd->tkd", fetch, returned)
        mixed = jnp.sum(gate_values[:, :, None] * chosen, axis=1).astype(BF)
        hidden = middle + join_columns(mixed)
        stored.append((attention_kept, routed, lookup, fetch, arrived, active, slope, chosen))

    expert_grads = None
    packs = [None] * layer_count
    tiny = [None] * layer_count
    incoming = cotangent.astype(F32)
    output = None
    for layer in reversed(range(layer_count)):
        if layer == layer_count - 1:
            middle, attention_kept = attention_forward(layer, hidden)
            routed = route(layer, middle)
            second_low, gate_values = routed[0], routed[5]
            lookup, fetch = slot_table(expert_ids[layer], experts, capacity)
            dispatch = ein("tc,td->cd", lookup[:, 0] + lookup[:, 1], second_low).astype(BF)
            back_send = slot_grads(lookup, gate_values, incoming)
            arrived = to_owners(dispatch, devices)
            out_grad = to_owners(back_send, devices)
            chunks, active, slope = run_forward(layer, arrived)
            back_chunks, pre_grad = expert_backward(
                layer, out_grad, slope, up_weight, down_weight
            )
            back = go_back(jnp.concatenate([chunks, back_chunks], axis=3))
            half = back.shape[2] // 2
            returned = summed_rows(back[:, :, :half], devices, shards)
            row_grad = summed_rows(back[:, :, half:], devices, shards)
            chosen = ein("tkc,cd->tkd", fetch, returned)
            mixed = jnp.sum(gate_values[:, :, None] * chosen, axis=1).astype(BF)
            output = middle + join_columns(mixed)
        else:
            attention_kept, routed, lookup, fetch, arrived, active, slope, chosen = stored[layer]
            back_send = slot_grads(lookup, routed[5], incoming)
            out_grad = to_owners(back_send, devices)
            back_chunks, pre_grad = expert_backward(
                layer, out_grad, slope, up_weight, down_weight
            )
            row_grad = summed_rows(go_back(back_chunks), devices, shards)
        expert_grads = expert_weights(
            layer, layer_count, arrived, out_grad, active, pre_grad, expert_grads
        )
        second_low, unit_two, inverse_two, router_prob, picked, gate_values = routed
        first_low, unit_one, inverse_one, queries, keys_low, values_low, weights, context = (
            attention_kept
        )
        gate_part = jnp.sum(own_columns(incoming)[:, None, :] * chosen, axis=2).T
        gate_grad = jnp.sum(gather_shard(gate_part), axis=0).T
        second_part = ein("tc,cd->td", fetch[:, 0] + fetch[:, 1], row_grad).astype(BF)
        prob_grad = jnp.sum(gate_grad[:, :, None] * picked, axis=1)
        logit_grad = (
            router_prob * (prob_grad - jnp.sum(gate_grad * gate_values, axis=1, keepdims=True))
        ).astype(BF)
        second_grad = join_columns(second_part) + ein(
            "te,de->td", logit_grad, router_weight[layer]
        )
        middle_grad = incoming + norm_backward(
            second_grad, unit_two, inverse_two, norm_gain[layer, 1].astype(F32)
        )
        mix_low = middle_grad.astype(BF)
        context_grad = ein("td,cd->tc", mix_low, output_weight[layer]).astype(BF)
        context_grad = context_grad.reshape(shape_three)
        weights_low = weights.astype(BF)
        prob_dot = ein("qhd,khd->hqk", context_grad, values_low)
        score_grad = (
            weights * (prob_dot - jnp.sum(weights * prob_dot, axis=2, keepdims=True))
        ).astype(BF)
        query_grad = ein("hqk,khd->qhd", score_grad, keys_low) * score_scale
        key_grad = ein("hqk,qhd->khd", score_grad, queries) * score_scale
        value_grad = ein("hqk,qhd->khd", weights_low, context_grad)
        parts = [
            part.astype(BF).reshape(token_count, local_width)
            for part in (query_grad, key_grad, value_grad)
        ]
        if layer == 0:
            *parts, last_total = lax.optimization_barrier((*parts, last_total))
        qkv_grad = jnp.concatenate(parts, axis=1)
        first_partial = (
            ein("tc,dc->td", parts[0], input_weight[layer, 0])
            + ein("tc,dc->td", parts[1], input_weight[layer, 1])
            + ein("tc,dc->td", parts[2], input_weight[layer, 2])
        )
        tiny[layer] = jnp.stack(
            [jnp.sum(first_partial * unit_one, axis=0), jnp.sum(first_partial, axis=0)]
        )
        blocks = jnp.pad(first_partial.astype(BF), ((0, rows_padded - token_count), (0, 0)))
        own_rows = sum_cycle(
            blocks.reshape(shards, row_block, width), "shard", me, shards, shard_pairs
        )

        def row_slice(value):
            padded = jnp.pad(value, ((0, rows_padded - token_count), (0, 0)))
            return lax.dynamic_slice_in_dim(padded, me * row_block, row_block, 0)

        norm_rows = norm_backward(
            own_rows,
            row_slice(unit_one),
            row_slice(inverse_one),
            norm_gain[layer, 0].astype(F32),
        )
        every = gather_shard(norm_rows.astype(BF)).reshape(rows_padded, width)
        packs[layer] = pack_of(
            second_low,
            logit_grad,
            second_grad,
            unit_two,
            middle_grad,
            mix_low,
            context,
            first_low,
            qkv_grad,
        )
        if layer == layer_count - 1:
            last_total = lax.psum(packs[layer], "expert")
        incoming = middle_grad + every[:token_count].astype(F32)

    cores = 2
    side = 4
    core, z_place, x_place = place % cores, (place // cores) % side, place // (cores * side)

    def core_pairs(step):
        return [(p, p ^ 1) for p in range(devices)]

    def z_pairs(step):
        return [
            (p, (p // 8) * 8 + ((p // 2 + step) % 4) * 2 + p % 2) for p in range(devices)
        ]

    def x_pairs(step):
        return [(p, ((p // 8 + step) % 4) * 8 + p % 8) for p in range(devices)]

    def sum_expert(value):
        columns = value.shape[1]
        chunk = value.shape[0] // devices
        blocks = value.reshape(side * side, cores, chunk, columns)
        mine = lax.dynamic_index_in_dim(blocks, core, 1, keepdims=False)
        away = lax.dynamic_index_in_dim(blocks, 1 - core, 1, keepdims=False)
        level = mine.astype(F32) + lax.ppermute(away, "expert", core_pairs(1)).astype(F32)
        level = level.astype(BF).reshape(side, side, chunk, columns)
        level = sum_cycle(level, "expert", x_place, side, x_pairs).astype(BF)
        level = sum_cycle(level, "expert", z_place, side, z_pairs).astype(BF)
        level = gather_cycle(level, "expert", z_place, side, z_pairs)
        level = gather_cycle(level, "expert", x_place, side, x_pairs)
        level = level.reshape(side * side, chunk, columns)
        other = lax.ppermute(level, "expert", core_pairs(1))
        level = jnp.where(
            core == 0, jnp.stack([level, other], axis=1), jnp.stack([other, level], axis=1)
        )
        return level.reshape(value.shape)

    small = jnp.concatenate(tiny, axis=0)
    small = jnp.sum(gather_shard(small), axis=0)
    small = small + lax.ppermute(small, "expert", core_pairs(1))
    small = jnp.sum(gather_cycle(small, "expert", x_place, side, x_pairs), axis=0)
    small = jnp.sum(gather_cycle(small, "expert", z_place, side, z_pairs), axis=0)
    totals = [sum_expert(packs[0]).astype(F32), last_total.astype(F32)]
    gain_list, shift_list, inw_list, inb_list, outw_list, outb_list, route_list = (
        [] for _ in range(7)
    )
    for layer in range(layer_count):
        total = totals[layer]
        inw_list.append(total[:, : 3 * local_width].reshape(width, 3, local_width).transpose(1, 0, 2))
        outw_list.append(total[:, 3 * local_width : width].T)
        route_list.append(total[:, width : width + experts])
        rest = total[:, width + experts :].T
        gain_list.append(jnp.stack([small[2 * layer], rest[0]]))
        shift_list.append(jnp.stack([small[2 * layer + 1], rest[1]]))
        outb_list.append(rest[2])
        inb_list.append(rest[3, : 2 * local_width].reshape(2, local_width))
    return (
        output,
        incoming,
        jnp.stack(gain_list),
        jnp.stack(shift_list),
        jnp.stack(inw_list),
        jnp.stack(inb_list),
        jnp.stack(outw_list),
        jnp.stack(outb_list),
        jnp.stack(route_list),
        *expert_grads,
    )


def solution(mesh):
    return jax.shard_map(
        body,
        mesh=mesh,
        in_specs=(
            P("expert", None),
            P(None, "expert", None),
            P(),
            P(),
            P(None, None, None, "shard"),
            P(None, None, "shard"),
            P(None, "shard", None),
            P(),
            P(),
            P(None, "expert", None, "shard"),
            P(None, "expert", "shard"),
            P(None, "expert", "shard", None),
            P(None, "expert", None),
            P("expert", None),
        ),
        out_specs=(
            P("expert", None),
            P("expert", None),
            P(),
            P(),
            P(None, None, None, "shard"),
            P(None, None, "shard"),
            P(None, "shard", None),
            P(),
            P(),
            P(None, "expert", None, "shard"),
            P(None, "expert", "shard"),
            P(None, "expert", "shard", None),
            P(None, "expert", None),
        ),
        check_vma=False,
    )
```

```python
import functools

import jax
import jax.numpy as jnp
from jax import lax
from jax.experimental import pallas as pl
from jax.experimental.pallas import tpu as pltpu
from jax.sharding import PartitionSpec as P

HEAD = 64
BF = jnp.bfloat16
F32 = jnp.float32

eps = 1e-06


def dot(left, right):
    return jnp.dot(left, right, preferred_element_type=F32)


def dot_nt(left, right):
    return lax.dot_general(left, right, (((1,), (1,)), ((), ())), preferred_element_type=F32)


def dot_tn(left, right):
    return lax.dot_general(left, right, (((0,), (0,)), ((), ())), preferred_element_type=F32)


def normalized(values):
    centred = values - jnp.mean(values, axis=1, keepdims=True)
    inverse = lax.rsqrt(jnp.mean(centred * centred, axis=1, keepdims=True) + eps)
    return centred * inverse, inverse


def norm_backward(incoming, normed, inverse, gain_row):
    scaled = incoming * gain_row
    return inverse * (
        scaled
        - jnp.mean(scaled, axis=1, keepdims=True)
        - normed * jnp.mean(scaled * normed, axis=1, keepdims=True)
    )


def softmax_rows(scores):
    raised = jnp.exp(scores - jnp.max(scores, axis=1, keepdims=True))
    return raised / jnp.sum(raised, axis=1, keepdims=True)


def one_hot(column, size):
    places = lax.broadcasted_iota(jnp.int32, (column.shape[0], size), 1)
    return places == column


def low(mask):
    return mask.astype(F32).astype(BF)


def row_of(ref, layer, row):
    return ref[...].astype(F32)[layer][row : row + 1]


def in_order(me, place, count):
    return lax.rem(me + count - place, count)


def folded(values, extra=None):
    rows, lanes = values.shape
    half = 8 * (-(-rows // 16))
    padding = jnp.zeros((2 * half - rows, lanes), F32)
    values = jnp.concatenate([values.astype(F32), padding], axis=0)
    sides = [jnp.concatenate([values[:half], values[half:]], axis=1)]
    if extra is not None:
        sides.append(extra)
    return jnp.concatenate(sides, axis=0).astype(BF)


def unfolded(values, rows):
    half, lanes = 8 * (-(-rows // 16)), values.shape[1] // 2
    values = values[:half]
    return jnp.concatenate([values[:, :lanes], values[:, lanes:]], axis=0)[:rows]


def joined_columns(parts_ref, me, count, rows):
    parts = [
        unfolded(parts_ref[in_order(me, j, count)].astype(F32), rows) for j in range(count)
    ]
    share = parts[0].shape[1]
    tile = 2 * share // 3
    return jnp.concatenate(
        [part[:, :tile] for part in parts] + [part[:, tile:] for part in parts], axis=1
    )


def attention_kernel(layer, joins, me_ref, hidden_ref, *rest):
    parts, rest = rest[:joins], rest[joins:]
    gain_ref, shift_ref, weight_ref, bias_ref, first_ref, qkv_ref, context_ref, fold_ref = rest[:8]
    hidden = hidden_ref[...].astype(F32)
    if joins:
        hidden_out, scratch = rest[8:]
        for step in range(joins):
            scratch[step] = parts[step][...]
        hidden = hidden + joined_columns(scratch, me_ref[0], joins, hidden.shape[0])
        hidden_out[...] = hidden
    unit, _ = normalized(hidden)
    first_low = (unit * row_of(gain_ref, layer, 0) + row_of(shift_ref, layer, 0)).astype(BF)
    first_ref[...] = first_low
    bias = bias_ref[...].astype(F32)[layer]
    queries = (dot_nt(first_low, weight_ref[0, 0]) + bias[0:1]).astype(BF)
    keys_low = dot_nt(first_low, weight_ref[0, 1]).astype(BF)
    values_low = (dot_nt(first_low, weight_ref[0, 2]) + bias[1:2]).astype(BF)
    qkv_ref[0] = queries
    qkv_ref[1] = keys_low
    qkv_ref[2] = values_low
    contexts = []
    for head in range(queries.shape[1] // HEAD):
        lanes = slice(head * HEAD, (head + 1) * HEAD)
        scores = dot_nt(queries[:, lanes], keys_low[:, lanes]) * (HEAD ** (-0.5))
        contexts.append(dot(softmax_rows(scores).astype(BF), values_low[:, lanes]))
    context = jnp.concatenate(contexts, axis=1).astype(BF)
    context_ref[...] = context
    fold_ref[...] = folded(context)


def route_kernel(layer, capacity, me_ref, hidden_ref, *rest):
    parts, rest = rest[:4], rest[4:]
    out_ref, out_bias_ref, gain_ref, shift_ref, router_ref, ids_ref = rest[:6]
    middle_ref, second_ref, prob_ref, gate_ref, column_ref, send_ref, scratch = rest[6:]
    count = len(parts)
    for step in range(count):
        scratch[step] = parts[step][...]
    tokens = hidden_ref.shape[0]
    mix = None
    for j in range(count):
        context = unfolded(scratch[in_order(me_ref[0], j, count)].astype(F32), tokens).astype(BF)
        part = dot(context, out_ref[j])
        mix = part if mix is None else mix + part
    middle = hidden_ref[...].astype(F32) + mix + out_bias_ref[...].astype(F32)[layer : layer + 1]
    middle_ref[...] = middle
    unit, _ = normalized(middle)
    second_low = (unit * row_of(gain_ref, layer, 1) + row_of(shift_ref, layer, 1)).astype(BF)
    second_ref[...] = second_low
    prob = softmax_rows(dot_nt(second_low, router_ref[layer]))
    prob_ref[...] = prob
    ids = ids_ref[layer]
    experts = prob.shape[1]
    picks = [one_hot(ids[:, k : k + 1], experts) for k in range(2)]
    before = lax.broadcasted_iota(jnp.int32, (tokens, tokens), 0) > lax.broadcasted_iota(
        jnp.int32, (tokens, tokens), 1
    )
    named = low(jnp.logical_or(picks[0], picks[1]))
    earlier = dot(low(before), named)
    columns = []
    for k in range(2):
        gate_ref[:, k : k + 1] = jnp.sum(jnp.where(picks[k], prob, 0.0), axis=1, keepdims=True)
        slot = jnp.sum(jnp.where(picks[k], earlier, 0.0), axis=1, keepdims=True)
        columns.append(ids[:, k : k + 1] * capacity + slot.astype(jnp.int32))
        column_ref[:, k : k + 1] = columns[k]
    slots = experts * capacity
    lookup = jnp.logical_or(one_hot(columns[0], slots), one_hot(columns[1], slots))
    send_ref[...] = dot_tn(low(lookup), second_low).astype(BF)


def send_kernel(joins, me_ref, base_ref, *rest):
    parts, rest = rest[:joins], rest[joins:]
    gate_ref, column_ref, send_ref = rest[:3]
    incoming = base_ref[...].astype(F32)
    if joins:
        incoming_out, scratch = rest[3:]
        rows = parts[0].shape[0]
        for step in range(joins):
            start = pl.multiple_of(in_order(me_ref[0], step, joins) * rows, 8)
            scratch[pl.ds(start, rows)] = parts[step][...].astype(F32)
        incoming = incoming + scratch[0 : incoming.shape[0]]
        incoming_out[...] = incoming
    slots = send_ref.shape[0]
    total = None
    for k in range(2):
        scaled = (gate_ref[:, k : k + 1] * incoming).astype(BF)
        part = dot_tn(low(one_hot(column_ref[:, k : k + 1], slots)), scaled)
        total = part if total is None else total + part
    send_ref[...] = total.astype(BF)


def combine_kernel(has_out, has_back, capacity, me_ref, arrived_ref, gate_ref, column_ref, *rest):
    devices, shards, half, _ = arrived_ref.shape
    rest = list(rest)
    incoming_ref = rest.pop(0) if has_back else None
    kept_ref = rest.pop(0) if not has_out else None
    share = 2 * (arrived_ref.shape[3] // (2 if has_out and has_back else 1)) // 4
    tile = 2 * share // 3
    rows = devices * half
    columns = [column_ref[:, k : k + 1] for k in range(2)]
    upper = [lax.rem(column, capacity) >= half for column in columns]
    fetch = [
        low(one_hot(lax.div(column, capacity) * half + lax.rem(column, half), rows))
        for column in columns
    ]

    def taken(first):
        lanes = slice(first, first + 2 * share)
        total = arrived_ref[:, 0, :, lanes].astype(F32)
        for j in range(1, shards):
            total = total + arrived_ref[:, j, :, lanes].astype(F32)
        table = total.reshape(rows, 2 * share).astype(BF)
        chosen = []
        for k in range(2):
            found = dot(fetch[k], table)
            mixed = found[:, 2 * tile :]
            lower = jnp.concatenate([found[:, :tile], mixed[:, : tile // 2]], axis=1)
            higher = jnp.concatenate([found[:, tile : 2 * tile], mixed[:, tile // 2 :]], axis=1)
            chosen.append(jnp.where(upper[k], higher, lower))
        return chosen

    if has_out:
        mixed_ref = rest.pop(0)
        chosen = taken(0)
        mixed_ref[...] = folded(gate_ref[:, 0:1] * chosen[0] + gate_ref[:, 1:2] * chosen[1])
        if not has_back:
            kept_out = rest.pop(0)
            for k in range(2):
                kept_out[k] = chosen[k].astype(BF)
    else:
        chosen = [kept_ref[k].astype(F32) for k in range(2)]
    if has_back:
        back_ref = rest.pop(0)
        found = taken(2 * share if has_out else 0)
        me = me_ref[0]
        first = incoming_ref[:, pl.ds(pl.multiple_of(me * tile, tile), tile)]
        start = pl.multiple_of((shards + lax.div(me, 2)) * tile, tile)
        last = incoming_ref[:, pl.ds(start, tile)]
        last = jnp.where(lax.rem(me, 2) == 0, last[:, : tile // 2], last[:, tile // 2 :])
        own = jnp.concatenate([first, last], axis=1).astype(F32)
        tokens = own.shape[0]
        lanes = lax.broadcasted_iota(jnp.int32, (2 * share, 128), 1)
        wide = jnp.zeros((2 * share, 128), F32)
        for k in range(2):
            gate_grad = jnp.sum(own * chosen[k], axis=1, keepdims=True)
            gate_grad = jnp.concatenate(
                [gate_grad, jnp.zeros((2 * share - tokens, 1), F32)], axis=0
            )
            upper_bits = gate_grad.astype(BF).astype(F32)
            wide = jnp.where(lanes == k, upper_bits, wide)
            wide = jnp.where(lanes == 2 + k, gate_grad - upper_bits, wide)
        back_ref[...] = folded(found[0] + found[1], wide.T[0:8])


def backward_block_kernel(layer, share, block, me_ref, incoming_ref, *rest):
    parts, rest = rest[:4], rest[4:]
    middle_ref, hidden_ref, prob_ref, gate_ref, ids_ref, qkv_ref = rest[:6]
    gain_ref, router_ref, out_weight_ref, weight_ref = rest[6:10]
    dh_ref, dqkv_ref, dz_ref, dlogit_ref, rows_ref = rest[10:15]
    block_refs = rest[15:19]
    unit_ref, inverse_ref, scratch, padded = rest[19:]
    me = me_ref[0]
    count = len(parts)
    for step in range(count):
        scratch[step] = parts[step][...]
    tokens = incoming_ref.shape[0]
    second_grad = joined_columns(scratch, me, count, tokens)
    gates = None
    for j in range(count):
        tail = scratch[in_order(me, j, count)].astype(F32)
        tail = tail[tail.shape[0] - 8 :]
        gates = tail if gates is None else gates + tail
    gates = jnp.concatenate([gates, jnp.zeros((120, gates.shape[1]), F32)], axis=0).T
    gates = (gates[:, 0:2] + gates[:, 2:4])[:tokens]
    prob = prob_ref[...]
    ids = ids_ref[layer]
    scaled = gates * gate_ref[...]
    prob_grad = jnp.zeros_like(prob)
    for k in range(2):
        prob_grad = prob_grad + jnp.where(
            one_hot(ids[:, k : k + 1], prob.shape[1]), gates[:, k : k + 1], 0.0
        )
    dlogit = (prob * (prob_grad - (scaled[:, 0:1] + scaled[:, 1:2]))).astype(BF)
    dlogit_ref[...] = dlogit
    second_grad = second_grad + dot(dlogit, router_ref[layer])
    unit_two, inverse_two = normalized(middle_ref[...])
    dh = incoming_ref[...].astype(F32) + norm_backward(
        second_grad, unit_two, inverse_two, row_of(gain_ref, layer, 1)
    )
    dh_ref[...] = dh
    dz = dh.astype(BF)
    dz_ref[...] = dz
    context_grad = dot_nt(dz, out_weight_ref[0]).astype(BF)
    queries, keys_low, values_low = qkv_ref[0], qkv_ref[1], qkv_ref[2]
    scale = HEAD ** (-0.5)
    grads = [[], [], []]
    for head in range(queries.shape[1] // HEAD):
        lanes = slice(head * HEAD, (head + 1) * HEAD)
        query, key, value = queries[:, lanes], keys_low[:, lanes], values_low[:, lanes]
        outer = context_grad[:, lanes]
        weights = softmax_rows(dot_nt(query, key) * scale)
        prob_dot = dot_nt(outer, value)
        score_grad = (
            weights * (prob_dot - jnp.sum(weights * prob_dot, axis=1, keepdims=True))
        ).astype(BF)
        grads[0].append(dot(score_grad, key) * scale)
        grads[1].append(dot_tn(score_grad, query) * scale)
        grads[2].append(dot_tn(weights.astype(BF), outer))
    partial = None
    sums = []
    for i in range(3):
        grad = jnp.concatenate(grads[i], axis=1).astype(BF)
        dqkv_ref[i] = grad
        sums.append(jnp.sum(grad.astype(F32), axis=0, keepdims=True))
        part = dot(grad, weight_ref[0, i])
        partial = part if partial is None else partial + part
    unit_one, inverse_one = normalized(hidden_ref[...].astype(F32))
    width = partial.shape[1]
    rows_ref[...] = jnp.zeros_like(rows_ref)
    rows_ref[0:1] = jnp.sum(second_grad * unit_two, axis=0, keepdims=True)
    rows_ref[1:2] = jnp.sum(second_grad, axis=0, keepdims=True)
    rows_ref[2:3] = jnp.sum(dh, axis=0, keepdims=True)
    rows_ref[3:4] = jnp.concatenate(
        [sums[0], sums[2], jnp.zeros((1, width - 2 * share), F32)], axis=1
    )
    rows_ref[4:5] = jnp.sum(partial * unit_one, axis=0, keepdims=True)
    rows_ref[5:6] = jnp.sum(partial, axis=0, keepdims=True)

    def spread_rows(values):
        padded[...] = jnp.zeros_like(padded)
        padded[0:tokens] = values

    def rows_of(step):
        start = pl.multiple_of(lax.rem(me + step, count) * block, 8)
        return padded[pl.ds(start, block)]

    spread_rows(partial)
    for step in range(count):
        block_refs[step][...] = rows_of(step).astype(BF)
    spread_rows(unit_one)
    unit_ref[...] = rows_of(0)
    spread_rows(jnp.broadcast_to(inverse_one, partial.shape))
    inverse_ref[...] = rows_of(0)[:, 0:128]


def norm_rows_kernel(layer, p0, p1, p2, p3, unit_ref, inverse_ref, gain_ref, out_ref):
    total = p0[...].astype(F32) + p1[...].astype(F32) + p2[...].astype(F32) + p3[...].astype(F32)
    out_ref[...] = norm_backward(
        total, unit_ref[...], inverse_ref[:, 0:1], row_of(gain_ref, layer, 0)
    ).astype(BF)


def pack_kernel(first_ref, dqkv_ref, context_ref, dz_ref, second_ref, dlogit_ref, rows_ref, core_ref, mine_ref, away_ref, target):
    width = first_ref.shape[1]
    share = dqkv_ref.shape[2]
    experts = dlogit_ref.shape[1]
    half = (width + experts) // 2
    size = target.shape[0] // 2
    gap = size - half

    def put(start, values):
        stop = start + values.shape[0]
        if stop <= half:
            target[start:stop] = values
        elif start >= half:
            target[start + gap : stop + gap] = values
        else:
            target[start:half] = values[: half - start]
            target[size : stop + gap] = values[half - start :]

    first_low = first_ref[...]
    for i in range(3):
        put(i * share, dot_tn(dqkv_ref[i], first_low))
    put(3 * share, dot_tn(context_ref[...], dz_ref[...]))
    put(width, dot_tn(dlogit_ref[...], second_ref[...]))
    small = jnp.concatenate([rows_ref[...], jnp.zeros((gap - 8, width), F32)], axis=0)
    target[half:size] = small
    target[size + half :] = small
    core = core_ref[0]
    mine_ref[...] = target[pl.ds(pl.multiple_of(core * size, 8), size)].astype(BF)
    away_ref[...] = target[pl.ds(pl.multiple_of((1 - core) * size, 8), size)].astype(BF)


def sum_kernel(count, pieces, index_ref, *rest):
    parts, outs, scratch = rest[:count], rest[count : count + pieces], rest[-1]
    total = parts[0][...].astype(F32)
    for part in parts[1:]:
        total = total + part[...].astype(F32)
    if pieces == 1:
        outs[0][...] = total.astype(BF)
        return
    rows = outs[0].shape[0]
    scratch[0 : total.shape[0]] = total
    if scratch.shape[0] > total.shape[0]:
        scratch[total.shape[0] :] = jnp.zeros(
            (scratch.shape[0] - total.shape[0], total.shape[1]), F32
        )
    for step in range(pieces):
        start = pl.multiple_of(lax.rem(index_ref[0] + step, pieces) * rows, 8)
        outs[step][...] = scratch[pl.ds(start, rows)].astype(BF)


def order_kernel(count, index_ref, *rest):
    parts, out_ref, scratch = rest[:count], rest[count], rest[count + 1]
    rows = parts[0].shape[0]
    for step in range(count):
        start = pl.multiple_of(in_order(index_ref[0], step, count) * rows, 8)
        scratch[pl.ds(start, rows)] = parts[step][...].astype(F32)
    out_ref[...] = scratch[0 : out_ref.shape[0]].astype(BF)


def add_rows_kernel(count, me_ref, base_ref, *rest):
    parts, out_ref, scratch = rest[:count], rest[count], rest[count + 1]
    rows = parts[0].shape[0]
    for step in range(count):
        start = pl.multiple_of(in_order(me_ref[0], step, count) * rows, 8)
        scratch[pl.ds(start, rows)] = parts[step][...].astype(F32)
    out_ref[...] = base_ref[...] + scratch[0 : out_ref.shape[0]]


def add_columns_kernel(count, me_ref, base_ref, *rest):
    parts, out_ref, scratch = rest[:count], rest[count], rest[count + 1]
    for step in range(count):
        scratch[step] = parts[step][...]
    out_ref[...] = base_ref[...] + joined_columns(scratch, me_ref[0], count, out_ref.shape[0])


def unpack_kernel(core_ref, me_ref, *rest):
    levels, smalls, outs = rest[:4], rest[4:8], rest[8:12]
    scratch, small_scratch = rest[12:]
    inw_ref, outw_ref, route_ref, rows_ref = outs
    size = levels[0].shape[0]
    core = core_ref[0]
    share, width = inw_ref.shape[2], inw_ref.shape[3]
    experts = route_ref.shape[1]
    half = (width + experts) // 2
    gap = size - half
    count = len(smalls)
    for step in range(count):
        small_scratch[step] = smalls[step][...].astype(F32)
    small = small_scratch[in_order(me_ref[0], 0, count)]
    for j in range(1, count):
        small = small + small_scratch[in_order(me_ref[0], j, count)]
    for layer in range(2):
        mine_ref, other_ref = levels[2 * layer], levels[2 * layer + 1]
        scratch[pl.ds(pl.multiple_of(core * size, 8), size)] = mine_ref[...].astype(F32)
        scratch[pl.ds(pl.multiple_of((1 - core) * size, 8), size)] = other_ref[...].astype(F32)

        def rows(start, stop):
            if stop <= half:
                return scratch[start:stop]
            if start >= half:
                return scratch[start + gap : stop + gap]
            return jnp.concatenate([scratch[start:half], scratch[size : stop + gap]], axis=0)

        for i in range(3):
            inw_ref[layer, i] = rows(i * share, (i + 1) * share)
        outw_ref[layer] = rows(3 * share, width)
        route_ref[layer] = rows(width, width + experts)
        rows_ref[layer, 0:4] = scratch[half : half + 4]
        rows_ref[layer, 4:8] = small[8 * layer + 4 : 8 * layer + 8]


def write_chunks(total, out_ref):
    devices, _, half, _ = out_ref.shape
    rows = total.reshape(devices, 2 * half, total.shape[1])
    lower, upper = rows[:, :half], rows[:, half:]
    tile = total.shape[1] // 6
    part = tile // 2
    for j in range(4):
        first = slice(j * tile, (j + 1) * tile)
        rest = slice(4 * tile + j * part, 4 * tile + (j + 1) * part)
        mixed = jnp.concatenate([lower[:, :, rest], upper[:, :, rest]], axis=2)
        block = jnp.concatenate([lower[:, :, first], upper[:, :, first], mixed], axis=2)
        out_ref[:, j, :, out_ref.shape[3] - 3 * tile :] = block.astype(BF)


def forward_kernel(layer, me_ref, x_ref, up_ref, up_bias_ref, down_ref, down_bias_ref, chunk_ref, active_ref, slope_ref, total):
    step = pl.program_id(0)
    rows = x_ref[...].reshape(total.shape)
    pre = jnp.dot(rows, up_ref[0, 0], preferred_element_type=F32)
    pre = pre + up_bias_ref[...].astype(F32)[0, layer : layer + 1]
    half_cdf = 0.5 * (1.0 + lax.erf(pre * 0.7071067811865476))
    active = (pre * half_cdf).astype(BF)
    active_ref[...] = active
    slope_ref[...] = half_cdf + pre * jnp.exp(-0.5 * pre * pre) * 0.3989422804014327
    part = jnp.dot(active, down_ref[0, 0], preferred_element_type=F32)

    @pl.when(step == 0)
    def _():
        offset = down_bias_ref[...].astype(F32)[0, layer : layer + 1]
        total[...] = part + jnp.where(me_ref[0] == 0, offset, 0.0)

    @pl.when(step > 0)
    def _():
        total[...] += part

    @pl.when(step == pl.num_programs(0) - 1)
    def _():
        write_chunks(total[...], chunk_ref)


def backward_kernel(joins, dy_ref, slope_ref, up_ref, down_ref, *rest):
    chunk_ref, pre_grad_ref, total = rest[joins:]
    step = pl.program_id(0)
    out_grad = dy_ref[...].reshape(total.shape)
    pre_grad = (dot_nt(out_grad, down_ref[0, 0]) * slope_ref[...]).astype(BF)
    pre_grad_ref[...] = pre_grad
    part = dot_nt(pre_grad, up_ref[0, 0])

    @pl.when(step == 0)
    def _():
        total[...] = part

    @pl.when(step > 0)
    def _():
        total[...] += part

    @pl.when(step == pl.num_programs(0) - 1)
    def _():
        if joins:
            chunk_ref[:, :, :, : rest[0].shape[3]] = rest[0][...]
        write_chunks(total[...], chunk_ref)


def weight_kernel(x_ref, dy_ref, active_ref, pre_grad_ref, *rest):
    up_ref, up_bias_ref, down_ref, down_bias_ref = rest[-4:]
    shape = active_ref.shape[0], x_ref.shape[2]
    pre_grad = pre_grad_ref[...]
    out_grad = dy_ref[...].reshape(shape)
    up_ref[0, 0] = dot_tn(x_ref[...].reshape(shape), pre_grad)
    down_ref[0, 0] = dot_tn(active_ref[...], out_grad)
    up_bias_ref[0] = jnp.sum(pre_grad.astype(F32), axis=0, keepdims=True)

    @pl.when(pl.program_id(0) == 0)
    def _():
        down_bias_ref[0] = jnp.sum(out_grad.astype(F32), axis=0, keepdims=True)


FBLOCK = 256
PARAMS = dict(vmem_limit_bytes=48 * 1024 * 1024)


def smem():
    return pl.BlockSpec(memory_space=pltpu.SMEM)


def near_out(shape, kind):
    return jax.ShapeDtypeStruct(shape, kind)


def far_out(shape, kind):
    return pltpu.HBM(shape, kind)


def far(value):
    return pltpu.with_memory_space_constraint(value, pltpu.HBM)


def call(kernel, name, outs, operands, scratch=(), specs=None):
    specs = specs or {}
    in_specs = [
        specs.get(i, smem() if operand.shape == (1,) else whole(operand.shape))
        for i, operand in enumerate(operands)
    ]
    return pl.pallas_call(
        kernel,
        grid=(1,),
        in_specs=in_specs,
        out_specs=[whole(out.shape) for out in outs],
        out_shape=outs,
        scratch_shapes=[pltpu.VMEM(shape, kind) for shape, kind in scratch],
        compiler_params=pltpu.CompilerParams(**PARAMS),
        name=name,
    )(*operands)


def layer_block(array, layer):
    shape = (1,) + array.shape[1:]
    return pl.BlockSpec(shape, lambda step: (layer,) + (0,) * (len(shape) - 1))


def whole(shape):
    return pl.BlockSpec(shape, lambda step: (0,) * len(shape))


def expert_forward(layer, me_one, arrived, up_weight, up_bias, down_weight, down_bias):
    devices, slots, width = arrived.shape
    hidden = up_weight.shape[3]
    rows = devices * slots
    return pl.pallas_call(
        functools.partial(forward_kernel, layer),
        grid=(hidden // FBLOCK,),
        in_specs=[
            smem(),
            whole(arrived.shape),
            pl.BlockSpec((1, 1, width, FBLOCK), lambda step: (layer, 0, 0, step)),
            pl.BlockSpec((1, up_bias.shape[1], FBLOCK), lambda step: (0, 0, step)),
            pl.BlockSpec((1, 1, FBLOCK, width), lambda step: (layer, 0, step, 0)),
            whole(down_bias.shape),
        ],
        out_specs=[
            whole((devices, 4, slots // 2, width // 2)),
            pl.BlockSpec((rows, FBLOCK), lambda step: (0, step)),
            pl.BlockSpec((rows, FBLOCK), lambda step: (0, step)),
        ],
        out_shape=[
            jax.ShapeDtypeStruct((devices, 4, slots // 2, width // 2), BF),
            pltpu.HBM((rows, hidden), BF),
            pltpu.HBM((rows, hidden), F32),
        ],
        scratch_shapes=[pltpu.VMEM((rows, width), F32)],
        compiler_params=pltpu.CompilerParams(**PARAMS),
        name="expert_forward",
    )(me_one, arrived, *map(far, (up_weight, up_bias, down_weight, down_bias)))


def expert_backward(layer, out_grad, slope, up_weight, down_weight, earlier=()):
    devices, slots, width = out_grad.shape
    hidden = up_weight.shape[3]
    rows = devices * slots
    chunk = (devices, 4, slots // 2, (1 + len(earlier)) * (width // 2))
    return pl.pallas_call(
        functools.partial(backward_kernel, len(earlier)),
        grid=(hidden // FBLOCK,),
        in_specs=[
            whole(out_grad.shape),
            pl.BlockSpec((rows, FBLOCK), lambda step: (0, step)),
            pl.BlockSpec((1, 1, width, FBLOCK), lambda step: (layer, 0, 0, step)),
            pl.BlockSpec((1, 1, FBLOCK, width), lambda step: (layer, 0, step, 0)),
        ]
        + [whole(value.shape) for value in earlier],
        out_specs=[whole(chunk), pl.BlockSpec((rows, FBLOCK), lambda step: (0, step))],
        out_shape=[jax.ShapeDtypeStruct(chunk, BF), pltpu.HBM((rows, hidden), BF)],
        scratch_shapes=[pltpu.VMEM((rows, width), F32)],
        compiler_params=pltpu.CompilerParams(**PARAMS),
        name="expert_backward",
    )(out_grad, *map(far, (slope, up_weight, down_weight, *earlier)))


def expert_weights(layer, layers, arrived, out_grad, active, pre_grad, earlier):
    devices, slots, width = out_grad.shape
    rows, hidden = active.shape
    operands = [*map(far, (arrived, out_grad, active, pre_grad))] + list(earlier or ())
    return pl.pallas_call(
        weight_kernel,
        grid=(hidden // FBLOCK,),
        in_specs=[
            whole(arrived.shape),
            whole(out_grad.shape),
            pl.BlockSpec((rows, FBLOCK), lambda step: (0, step)),
            pl.BlockSpec((rows, FBLOCK), lambda step: (0, step)),
        ]
        + [pl.BlockSpec(memory_space=pl.ANY)] * len(earlier or ()),
        out_specs=[
            pl.BlockSpec((1, 1, width, FBLOCK), lambda step: (layer, 0, 0, step)),
            pl.BlockSpec((1, 1, FBLOCK), lambda step: (layer, 0, step)),
            pl.BlockSpec((1, 1, FBLOCK, width), lambda step: (layer, 0, step, 0)),
            pl.BlockSpec((1, 1, width), lambda step: (layer, 0, 0)),
        ],
        out_shape=[
            pltpu.HBM((layers, 1, width, hidden), F32),
            pltpu.HBM((layers, 1, hidden), F32),
            pltpu.HBM((layers, 1, hidden, width), F32),
            pltpu.HBM((layers, 1, width), F32),
        ],
        input_output_aliases={4 + i: i for i in range(len(earlier or ()))},
        compiler_params=pltpu.CompilerParams(**PARAMS),
        name="expert_weights",
    )(*operands)


def cycle(size, step):
    return [(place, (place + step) % size) for place in range(size)]


def body(
    tokens,
    expert_ids,
    norm_gain,
    norm_bias,
    input_weight,
    input_bias,
    output_weight,
    output_bias,
    router_weight,
    up_weight,
    up_bias,
    down_weight,
    down_bias,
    cotangent,
):
    token_count, width = tokens.shape
    layer_count = norm_gain.shape[0]
    share = input_weight.shape[3]
    experts = router_weight.shape[2]
    devices = lax.axis_size("expert")
    shards = lax.axis_size("shard")
    capacity = 5 * token_count // (2 * experts) + 1
    slots = experts * capacity
    me = lax.axis_index("shard")
    place = lax.axis_index("expert")
    me_one = me.reshape(1)
    row_block = 8 * (-(-token_count // (8 * shards)))
    size = 32 * (-(-((width + experts) // 2 + 8) // 32))

    cores = 2
    side = 4
    core, z_place, x_place = place % cores, (place // cores) % side, place // (cores * side)
    core_one, z_one, x_one = core.reshape(1), z_place.reshape(1), x_place.reshape(1)

    def core_pairs():
        return [(p, p ^ 1) for p in range(devices)]

    def z_pairs(step):
        return [(p, (p // 8) * 8 + ((p // 2 + step) % 4) * 2 + p % 2) for p in range(devices)]

    def x_pairs(step):
        return [(p, ((p // 8 + step) % 4) * 8 + p % 8) for p in range(devices)]

    def spread(value):
        return [value] + [
            lax.ppermute(value, "shard", cycle(shards, step)) for step in range(1, shards)
        ]

    def exchange(blocks):
        return [blocks[0]] + [
            lax.ppermute(blocks[step], "shard", cycle(shards, step)) for step in range(1, shards)
        ]

    def gather_shard(value):
        stacked = jnp.stack(spread(value))
        return jnp.stack(
            [
                lax.dynamic_index_in_dim(stacked, (me - j) % shards, 0, keepdims=False)
                for j in range(shards)
            ]
        )

    def to_owners(rows):
        outgoing = rows.reshape(devices, capacity, width)
        return lax.all_to_all(outgoing, "expert", split_axis=0, concat_axis=0, tiled=True)

    def go_back(chunks):
        flat = chunks.reshape(-1, *chunks.shape[2:])
        back = lax.all_to_all(
            flat, ("expert", "shard"), split_axis=0, concat_axis=0, tiled=True
        )
        return back.reshape(chunks.shape)

    gains, shifts = far(norm_gain), far(norm_bias)
    in_bias, out_bias = far(input_bias), far(output_bias)
    up_rows, down_rows = jnp.swapaxes(up_bias, 0, 1), jnp.swapaxes(down_bias, 0, 1)
    ids = far(expert_ids)
    pair = (token_count, 2)
    square = (token_count, width)
    narrow = (token_count, share)
    fold_rows = 8 * (-(-token_count // 16))
    fold = (fold_rows, 2 * share)
    fold_more = (fold_rows + 8, 2 * share)
    in_weight = far(jnp.swapaxes(input_weight, 2, 3))
    router = far(jnp.swapaxes(router_weight, 1, 2))
    out_weight = far(output_weight)

    def attention_forward(layer, base, parts):
        joins = len(parts)
        operands = [me_one, base, *parts, gains, shifts, in_weight, in_bias]
        outs = [
            far_out(square, BF),
            far_out((3,) + narrow, BF),
            far_out(narrow, BF),
            near_out(fold, BF),
        ]
        scratch = []
        if joins:
            outs.append(far_out(square, F32))
            scratch.append(((joins,) + fold, BF))
        found = call(
            functools.partial(attention_kernel, layer, joins),
            "attention_forward",
            outs,
            operands,
            scratch,
            specs={joins + 4: layer_block(in_weight, layer)},
        )
        return found if joins else [*found, base]

    def route(layer, hidden, context_fold, gathered):
        return call(
            functools.partial(route_kernel, layer, capacity),
            "route",
            [
                far_out(square, F32),
                far_out(square, BF),
                far_out((token_count, experts), F32),
                far_out(pair, F32),
                far_out(pair, jnp.int32),
                near_out((slots, width), BF),
            ],
            [
                me_one,
                far(hidden),
                *spread(context_fold),
                gathered,
                out_bias,
                gains,
                shifts,
                router,
                ids,
            ],
            [((shards,) + fold, BF)],
        )

    def send_grads(base, parts, gate_values, columns):
        joins = len(parts)
        outs = [near_out((slots, width), BF)]
        scratch = []
        if joins:
            outs.append(far_out(square, F32))
            scratch.append(((joins * row_block, width), F32))
        return call(
            functools.partial(send_kernel, joins),
            "send_grads",
            outs,
            [me_one, base, *parts, far(gate_values), far(columns)],
            scratch,
        )

    def combine(arrived, gate_values, columns, incoming=None, kept=None):
        has_back, has_out = incoming is not None, kept is None
        outs = []
        if has_out:
            outs.append((far_out if has_back else near_out)(fold, BF))
            if not has_back:
                outs.append(far_out((2,) + narrow, BF))
        if has_back:
            outs.append(near_out(fold_more, BF))
        operands = [me_one, arrived, far(gate_values), far(columns)]
        operands += [far(value) for value in (incoming, kept) if value is not None]
        return call(
            functools.partial(combine_kernel, has_out, has_back, capacity),
            "combine",
            outs,
            operands,
        )

    def run_forward(layer, arrived):
        return expert_forward(layer, me_one, arrived, up_weight, up_rows, down_weight, down_rows)

    def block_backward(layer, incoming, parts, middle, hidden, prob, gate_values, qkv):
        block = near_out((row_block, width), BF)
        out = near_out if layer == 0 else far_out
        return call(
            functools.partial(backward_block_kernel, layer, share, row_block),
            "backward_block",
            [
                (far_out if layer == 0 else near_out)(square, F32),
                out((3,) + narrow, BF),
                out(square, BF),
                out((token_count, experts), BF),
                out((8, width), F32),
                block,
                block,
                block,
                block,
                near_out((row_block, width), F32),
                near_out((row_block, 128), F32),
            ],
            [
                me_one,
                far(incoming),
                *parts,
                far(middle),
                far(hidden),
                far(prob),
                far(gate_values),
                ids,
                far(qkv),
                gains,
                router,
                out_weight,
                in_weight,
            ],
            [((shards,) + fold_more, BF), ((shards * row_block, width), F32)],
            specs={
                14: layer_block(output_weight, layer),
                15: layer_block(in_weight, layer),
            },
        )

    def norm_rows(layer, blocks, unit, inverse):
        return call(
            functools.partial(norm_rows_kernel, layer),
            "norm_rows",
            [near_out((row_block, width), BF)],
            [*blocks, unit, inverse, gains],
        )[0]

    def pack(first_low, dqkv, context, dz, second_low, dlogit, rows):
        half = near_out((size, width), BF)
        return call(
            pack_kernel,
            "pack",
            [half, half],
            [first_low, dqkv, context, dz, second_low, dlogit, rows, core_one],
            [((2 * size, width), F32)],
        )

    quarter = size // side
    last = 8 * (-(-quarter // (8 * side)))

    def sums(parts, index, pieces, rows):
        return call(
            functools.partial(sum_kernel, len(parts), pieces),
            "sums",
            [near_out((rows, width), BF)] * pieces,
            [index, *parts],
            [((pieces * rows, width), F32)],
        )

    def ordered(parts, index, rows):
        return call(
            functools.partial(order_kernel, len(parts)),
            "ordered",
            [near_out((rows, width), BF)],
            [index, *parts],
            [((len(parts) * parts[0].shape[0], width), F32)],
        )[0]

    def sent(blocks, pairs):
        return [blocks[0]] + [
            lax.ppermute(blocks[step], "expert", pairs(step)) for step in range(1, side)
        ]

    def to_core(value):
        return lax.ppermute(value, "expert", core_pairs())

    def tied(*values):
        return lax.optimization_barrier(values)

    gathered = gather_shard(output_weight[0])
    first0, qkv0, context0, fold0, hidden0 = attention_forward(0, tokens, [])
    middle0, second0, prob0, gate0, column0, send = route(0, hidden0, fold0, gathered)
    send, later_weight = tied(send, output_weight[1])
    arrived0 = to_owners(send)
    later = spread(later_weight)
    arrived0, *later = tied(arrived0, *later)
    chunks, active0, slope0 = run_forward(0, arrived0)
    stacked = jnp.stack(later)
    gathered = jnp.stack(
        [
            lax.dynamic_index_in_dim(stacked, (me - j) % shards, 0, keepdims=False)
            for j in range(shards)
        ]
    )
    back, gathered = tied(go_back(chunks), gathered)
    mixed, kept0 = combine(back, gate0, column0)

    first1, qkv1, context1, fold1, hidden1 = attention_forward(1, far(middle0), spread(mixed))
    middle1, second1, prob1, gate1, column1, send = route(1, hidden1, fold1, gathered)
    (send_back,) = send_grads(far(cotangent), [], gate1, column1)
    arrived1 = to_owners(send)
    out_grad1 = to_owners(send_back)
    chunks, active1, slope1 = run_forward(1, arrived1)
    chunks, pre_grad1 = expert_backward(
        1, out_grad1, slope1, up_weight, down_weight, (chunks,)
    )
    back = go_back(chunks)
    expert_grads = expert_weights(
        1, layer_count, arrived1, out_grad1, active1, pre_grad1, None
    )
    back, *expert_grads = tied(back, *expert_grads)
    mixed, shares = combine(back, gate1, column1, incoming=cotangent)

    dh1, dqkv1, dz1, dlogit1, rows1, *blocks, unit, inverse = block_backward(
        1, cotangent, spread(shares), middle1, hidden1, prob1, gate1, qkv1
    )
    parts = spread(norm_rows(1, exchange(blocks), unit, inverse))
    send, incoming = send_grads(dh1, parts, gate0, column0)

    out_grad0 = to_owners(send)
    mine1, away1 = pack(*map(far, (first1, dqkv1, context1, dz1, second1, dlogit1, rows1)))
    away1 = to_core(away1)
    mixed = spread(mixed)
    output = call(
        functools.partial(add_columns_kernel, shards),
        "add_columns",
        [far_out(square, F32)],
        [me_one, far(middle1), *mixed],
        [((shards,) + fold, BF)],
    )[0]
    out_grad0, mine1, away1, output = tied(out_grad0, mine1, away1, output)
    back_chunks, pre_grad0 = expert_backward(0, out_grad0, slope0, up_weight, down_weight)
    back = go_back(back_chunks)
    level1 = sums([mine1, away1], x_one, side, quarter)
    expert_grads = expert_weights(
        0, layer_count, arrived0, out_grad0, active0, pre_grad0, expert_grads
    )
    back, *rest = tied(back, *level1, *expert_grads)
    level1, expert_grads = rest[:side], rest[side:]
    (shares,) = combine(back, gate0, column0, incoming=incoming, kept=kept0)
    level1 = sent(level1, x_pairs)
    shares = spread(shares)
    *shares, l0, l1, l2, l3 = tied(*shares, *level1)
    dh0, dqkv0, dz0, dlogit0, rows0, *blocks, unit, inverse = block_backward(
        0, incoming, shares, middle0, hidden0, prob0, gate0, qkv0
    )
    level1 = sent(sums([l0, l1, l2, l3], z_one, side, last), z_pairs)
    dqkv0, *level1 = tied(dqkv0, *level1)
    mine, away = pack(
        far(first0), dqkv0, far(context0), dz0, far(second0), dlogit0, rows0
    )
    away = to_core(away)

    level1 = sent(sums(level1, z_one, 1, last) * side, z_pairs)
    blocks = exchange(blocks)
    away, *rest = tied(away, *level1, *blocks)
    level1, blocks = rest[:side], rest[side:]
    level = sent(sums([mine, away], z_one, side, quarter), z_pairs)
    level1 = sent([ordered(level1, z_one, quarter)] * side, x_pairs)
    parts = spread(norm_rows(0, blocks, unit, inverse))
    level = tied(*level, *level1, *parts)
    level, level1, parts = level[:side], level[side : 2 * side], level[2 * side :]
    level = sent(sums(level, x_one, side, last), x_pairs)
    level1 = ordered(level1, x_one, size)
    other1 = to_core(level1)
    *level, level1, other1 = tied(*level, level1, other1)
    level = sent(sums(level, x_one, 1, last) * side, x_pairs)
    level = sent([ordered(level, x_one, quarter)] * side, z_pairs)
    level = ordered(level, z_one, size)
    other = to_core(level)
    half = (width + experts) // 2
    small = spread(jnp.concatenate([level[half : half + 8], level1[half : half + 8]], axis=0))
    grad_tokens = call(
        functools.partial(add_rows_kernel, shards),
        "add_rows",
        [far_out(square, F32)],
        [me_one, far(dh0), *parts],
        [((shards * row_block, width), F32)],
    )[0]
    inw, outw, router_grad, rows = call(
        unpack_kernel,
        "unpack",
        [
            far_out((layer_count, 3, share, width), F32),
            far_out((layer_count, share, width), F32),
            far_out((layer_count, experts, width), F32),
            near_out((layer_count, 8, width), F32),
        ],
        [core_one, me_one, level, other, level1, other1, *small],
        [((2 * size, width), F32), ((shards, 16, width), F32)],
    )
    return (
        output,
        grad_tokens,
        jnp.stack([rows[:, 4], rows[:, 0]], axis=1),
        jnp.stack([rows[:, 5], rows[:, 1]], axis=1),
        jnp.swapaxes(inw, 2, 3),
        rows[:, 3, : 2 * share].reshape(layer_count, 2, share),
        outw,
        rows[:, 2],
        jnp.swapaxes(router_grad, 1, 2),
        *expert_grads,
    )


def solution(mesh):
    return jax.shard_map(
        body,
        mesh=mesh,
        in_specs=(
            P("expert", None),
            P(None, "expert", None),
            P(),
            P(),
            P(None, None, None, "shard"),
            P(None, None, "shard"),
            P(None, "shard", None),
            P(),
            P(),
            P(None, "expert", None, "shard"),
            P(None, "expert", "shard"),
            P(None, "expert", "shard", None),
            P(None, "expert", None),
            P("expert", None),
        ),
        out_specs=(
            P("expert", None),
            P("expert", None),
            P(),
            P(),
            P(None, None, None, "shard"),
            P(None, None, "shard"),
            P(None, "shard", None),
            P(),
            P(),
            P(None, "expert", None, "shard"),
            P(None, "expert", "shard"),
            P(None, "expert", "shard", None),
            P(None, "expert", None),
        ),
        check_vma=False,
    )
```

```python
import functools

import jax
import jax.numpy as jnp
from jax import lax
from jax.experimental import pallas as pl
from jax.experimental.pallas import tpu as pltpu
from jax.sharding import PartitionSpec as P

HEAD = 64
BF = jnp.bfloat16
F32 = jnp.float32

eps = 1e-06


def dot(left, right):
    return jnp.dot(left, right, preferred_element_type=F32)


def dot_nt(left, right):
    return lax.dot_general(left, right, (((1,), (1,)), ((), ())), preferred_element_type=F32)


def dot_tn(left, right):
    return lax.dot_general(left, right, (((0,), (0,)), ((), ())), preferred_element_type=F32)


def normalized(values):
    centred = values - jnp.mean(values, axis=1, keepdims=True)
    inverse = lax.rsqrt(jnp.mean(centred * centred, axis=1, keepdims=True) + eps)
    return centred * inverse, inverse


def norm_backward(incoming, normed, inverse, gain_row):
    scaled = incoming * gain_row
    return inverse * (
        scaled
        - jnp.mean(scaled, axis=1, keepdims=True)
        - normed * jnp.mean(scaled * normed, axis=1, keepdims=True)
    )


def softmax_rows(scores):
    raised = jnp.exp(scores - jnp.max(scores, axis=1, keepdims=True))
    return raised / jnp.sum(raised, axis=1, keepdims=True)


def one_hot(column, size):
    places = lax.broadcasted_iota(jnp.int32, (column.shape[0], size), 1)
    return places == column


def low(mask):
    return mask.astype(F32).astype(BF)


def row_of(ref, layer, row):
    return ref[...].astype(F32)[layer][row : row + 1]


def in_order(me, place, count):
    return lax.rem(me + count - place, count)


def folded(values, extra=None):
    rows, lanes = values.shape
    half = 8 * (-(-rows // 16))
    padding = jnp.zeros((2 * half - rows, lanes), F32)
    values = jnp.concatenate([values.astype(F32), padding], axis=0)
    sides = [jnp.concatenate([values[:half], values[half:]], axis=1)]
    if extra is not None:
        sides.append(extra)
    return jnp.concatenate(sides, axis=0).astype(BF)


def unfolded(values, rows):
    half, lanes = 8 * (-(-rows // 16)), values.shape[1] // 2
    values = values[:half]
    return jnp.concatenate([values[:, :lanes], values[:, lanes:]], axis=0)[:rows]


def joined_columns(parts_ref, me, count, rows):
    parts = [
        unfolded(parts_ref[in_order(me, j, count)].astype(F32), rows) for j in range(count)
    ]
    share = parts[0].shape[1]
    tile = 2 * share // 3
    return jnp.concatenate(
        [part[:, :tile] for part in parts] + [part[:, tile:] for part in parts], axis=1
    )


def attention_kernel(layer, joins, me_ref, hidden_ref, *rest):
    parts, rest = rest[:joins], rest[joins:]
    gain_ref, shift_ref, weight_ref, bias_ref, first_ref, qkv_ref, context_ref, fold_ref = rest[:8]
    hidden = hidden_ref[...].astype(F32)
    if joins:
        hidden_out, scratch = rest[8:]
        for step in range(joins):
            scratch[step] = parts[step][...]
        hidden = hidden + joined_columns(scratch, me_ref[0], joins, hidden.shape[0])
        hidden_out[...] = hidden
    unit, _ = normalized(hidden)
    first_low = (unit * row_of(gain_ref, layer, 0) + row_of(shift_ref, layer, 0)).astype(BF)
    first_ref[...] = first_low
    bias = bias_ref[...].astype(F32)[layer]
    queries = (dot_nt(first_low, weight_ref[0, 0]) + bias[0:1]).astype(BF)
    keys_low = dot_nt(first_low, weight_ref[0, 1]).astype(BF)
    values_low = (dot_nt(first_low, weight_ref[0, 2]) + bias[1:2]).astype(BF)
    qkv_ref[0] = queries
    qkv_ref[1] = keys_low
    qkv_ref[2] = values_low
    contexts = []
    for head in range(queries.shape[1] // HEAD):
        lanes = slice(head * HEAD, (head + 1) * HEAD)
        scores = dot_nt(queries[:, lanes], keys_low[:, lanes]) * (HEAD ** (-0.5))
        contexts.append(dot(softmax_rows(scores).astype(BF), values_low[:, lanes]))
    context = jnp.concatenate(contexts, axis=1).astype(BF)
    context_ref[...] = context
    fold_ref[...] = folded(context)


def route_kernel(layer, capacity, me_ref, core_ref, hidden_ref, *rest):
    parts, rest = rest[:4], rest[4:]
    pieces, rest = rest[:7], rest[7:]
    out_bias_ref, gain_ref, shift_ref, router_ref, ids_ref = rest[:5]
    middle_ref, second_ref, prob_ref, gate_ref, column_ref, send_ref, scratch, out_ref = rest[5:]
    count = len(parts)
    part_rows = pieces[1].shape[0]
    near = pl.multiple_of(core_ref[0] * part_rows, 16)
    away = pl.multiple_of((1 - core_ref[0]) * part_rows, 16)
    out_ref[0] = pieces[0][0]
    for step in range(1, count):
        out_ref[step, pl.ds(near, part_rows)] = pieces[step][...]
        out_ref[step, pl.ds(away, part_rows)] = pieces[count - 1 + step][...]
    for step in range(count):
        scratch[step] = parts[step][...]
    tokens = hidden_ref.shape[0]
    mix = None
    for j in range(count):
        turn = in_order(me_ref[0], j, count)
        context = unfolded(scratch[turn].astype(F32), tokens).astype(BF)
        part = dot(context, out_ref[turn])
        mix = part if mix is None else mix + part
    middle = hidden_ref[...].astype(F32) + mix + out_bias_ref[...].astype(F32)[layer : layer + 1]
    middle_ref[...] = middle
    unit, _ = normalized(middle)
    second_low = (unit * row_of(gain_ref, layer, 1) + row_of(shift_ref, layer, 1)).astype(BF)
    second_ref[...] = second_low
    prob = softmax_rows(dot_nt(second_low, router_ref[layer]))
    prob_ref[...] = prob
    ids = ids_ref[layer]
    experts = prob.shape[1]
    picks, columns = slot_columns(ids, experts, capacity)
    for k in range(2):
        gate_ref[:, k : k + 1] = jnp.sum(jnp.where(picks[k], prob, 0.0), axis=1, keepdims=True)
        column_ref[:, k : k + 1] = columns[k]
    slots = experts * capacity
    lookup = jnp.logical_or(one_hot(columns[0], slots), one_hot(columns[1], slots))
    width = second_low.shape[1]
    send_ref[:, :width] = dot_tn(low(lookup), second_low).astype(BF)
    if send_ref.shape[1] > width:
        lanes = lax.broadcasted_iota(jnp.int32, (tokens, send_ref.shape[1] - width), 1)
        total = None
        for k in range(2):
            rest_bits = jnp.sum(jnp.where(picks[k], prob, 0.0), axis=1, keepdims=True)
            wide = jnp.zeros(lanes.shape, F32)
            for piece in range(3):
                bits = rest_bits.astype(BF).astype(F32)
                wide = jnp.where(lanes == piece, bits, wide)
                rest_bits = rest_bits - bits
            part = dot_tn(low(one_hot(columns[k], slots)), wide.astype(BF))
            total = part if total is None else total + part
        send_ref[:, width:] = total.astype(BF)


def slot_columns(ids, experts, capacity):
    tokens = ids.shape[0]
    picks = [one_hot(ids[:, k : k + 1], experts) for k in range(2)]
    before = lax.broadcasted_iota(jnp.int32, (tokens, tokens), 0) > lax.broadcasted_iota(
        jnp.int32, (tokens, tokens), 1
    )
    earlier = dot(low(before), low(jnp.logical_or(picks[0], picks[1])))
    columns = []
    for k in range(2):
        slot = jnp.sum(jnp.where(picks[k], earlier, 0.0), axis=1, keepdims=True)
        columns.append(ids[:, k : k + 1] * capacity + slot.astype(jnp.int32))
    return picks, columns


def early_kernel(layer, capacity, experts, ids_ref, rows_ref, send_ref):
    _, columns = slot_columns(ids_ref[layer], experts, capacity)
    slots = experts * capacity
    lookup = jnp.logical_or(one_hot(columns[0], slots), one_hot(columns[1], slots))
    send_ref[...] = dot_tn(low(lookup), rows_ref[...]).astype(BF)


def send_kernel(joins, me_ref, base_ref, *rest):
    parts, rest = rest[:joins], rest[joins:]
    gate_ref, column_ref, send_ref = rest[:3]
    incoming = base_ref[...].astype(F32)
    if joins:
        incoming_out, scratch = rest[3:]
        rows = parts[0].shape[0]
        for step in range(joins):
            start = pl.multiple_of(in_order(me_ref[0], step, joins) * rows, 8)
            scratch[pl.ds(start, rows)] = parts[step][...].astype(F32)
        incoming = incoming + scratch[0 : incoming.shape[0]]
        incoming_out[...] = incoming
    slots = send_ref.shape[0]
    total = None
    for k in range(2):
        scaled = (gate_ref[:, k : k + 1] * incoming).astype(BF)
        part = dot_tn(low(one_hot(column_ref[:, k : k + 1], slots)), scaled)
        total = part if total is None else total + part
    send_ref[...] = total.astype(BF)


def combine_kernel(has_out, has_back, capacity, me_ref, arrived_ref, gate_ref, column_ref, *rest):
    devices, shards, half, _ = arrived_ref.shape
    rest = list(rest)
    incoming_ref = rest.pop(0) if has_back else None
    kept_ref = rest.pop(0) if not has_out else None
    share = 2 * (arrived_ref.shape[3] // (2 if has_out and has_back else 1)) // 4
    tile = 2 * share // 3
    rows = devices * half
    columns = [column_ref[:, k : k + 1] for k in range(2)]
    upper = [lax.rem(column, capacity) >= half for column in columns]
    fetch = [
        low(one_hot(lax.div(column, capacity) * half + lax.rem(column, half), rows))
        for column in columns
    ]

    def taken(first):
        lanes = slice(first, first + 2 * share)
        total = arrived_ref[:, 0, :, lanes].astype(F32)
        for j in range(1, shards):
            total = total + arrived_ref[:, j, :, lanes].astype(F32)
        table = total.reshape(rows, 2 * share).astype(BF)
        chosen = []
        for k in range(2):
            found = dot(fetch[k], table)
            mixed = found[:, 2 * tile :]
            lower = jnp.concatenate([found[:, :tile], mixed[:, : tile // 2]], axis=1)
            higher = jnp.concatenate([found[:, tile : 2 * tile], mixed[:, tile // 2 :]], axis=1)
            chosen.append(jnp.where(upper[k], higher, lower))
        return chosen

    if has_out:
        mixed_ref = rest.pop(0)
        chosen = taken(0)
        mixed_ref[...] = folded(gate_ref[:, 0:1] * chosen[0] + gate_ref[:, 1:2] * chosen[1])
        if not has_back:
            kept_out = rest.pop(0)
            for k in range(2):
                kept_out[k] = chosen[k].astype(BF)
    else:
        chosen = [kept_ref[k].astype(F32) for k in range(2)]
    if has_back:
        back_ref = rest.pop(0)
        found = taken(2 * share if has_out else 0)
        me = me_ref[0]
        first = incoming_ref[:, pl.ds(pl.multiple_of(me * tile, tile), tile)]
        start = pl.multiple_of((shards + lax.div(me, 2)) * tile, tile)
        last = incoming_ref[:, pl.ds(start, tile)]
        last = jnp.where(lax.rem(me, 2) == 0, last[:, : tile // 2], last[:, tile // 2 :])
        own = jnp.concatenate([first, last], axis=1).astype(F32)
        tokens = own.shape[0]
        lanes = lax.broadcasted_iota(jnp.int32, (2 * share, 128), 1)
        wide = jnp.zeros((2 * share, 128), F32)
        for k in range(2):
            gate_grad = jnp.sum(own * chosen[k], axis=1, keepdims=True)
            gate_grad = jnp.concatenate(
                [gate_grad, jnp.zeros((2 * share - tokens, 1), F32)], axis=0
            )
            upper_bits = gate_grad.astype(BF).astype(F32)
            wide = jnp.where(lanes == k, upper_bits, wide)
            wide = jnp.where(lanes == 2 + k, gate_grad - upper_bits, wide)
        back_ref[...] = folded(found[0] + found[1], wide.T[0:8])


def backward_block_kernel(layer, share, block, me_ref, incoming_ref, *rest):
    parts, rest = rest[:4], rest[4:]
    middle_ref, hidden_ref, prob_ref, gate_ref, ids_ref, qkv_ref = rest[:6]
    gain_ref, router_ref, out_weight_ref, weight_ref = rest[6:10]
    dh_ref, dqkv_ref, dz_ref, dlogit_ref, rows_ref = rest[10:15]
    block_refs = rest[15:19]
    unit_ref, inverse_ref, scratch, padded = rest[19:]
    me = me_ref[0]
    count = len(parts)
    for step in range(count):
        scratch[step] = parts[step][...]
    tokens = incoming_ref.shape[0]
    second_grad = joined_columns(scratch, me, count, tokens)
    gates = None
    for j in range(count):
        tail = scratch[in_order(me, j, count)].astype(F32)
        tail = tail[tail.shape[0] - 8 :]
        gates = tail if gates is None else gates + tail
    gates = jnp.concatenate([gates, jnp.zeros((120, gates.shape[1]), F32)], axis=0).T
    gates = (gates[:, 0:2] + gates[:, 2:4])[:tokens]
    prob = prob_ref[...]
    ids = ids_ref[layer]
    scaled = gates * gate_ref[...]
    prob_grad = jnp.zeros_like(prob)
    for k in range(2):
        prob_grad = prob_grad + jnp.where(
            one_hot(ids[:, k : k + 1], prob.shape[1]), gates[:, k : k + 1], 0.0
        )
    dlogit = (prob * (prob_grad - (scaled[:, 0:1] + scaled[:, 1:2]))).astype(BF)
    dlogit_ref[...] = dlogit
    second_grad = second_grad + dot(dlogit, router_ref[layer])
    unit_two, inverse_two = normalized(middle_ref[...])
    dh = incoming_ref[...].astype(F32) + norm_backward(
        second_grad, unit_two, inverse_two, row_of(gain_ref, layer, 1)
    )
    dh_ref[...] = dh
    dz = dh.astype(BF)
    dz_ref[...] = dz
    context_grad = dot_nt(dz, out_weight_ref[0]).astype(BF)
    queries, keys_low, values_low = qkv_ref[0], qkv_ref[1], qkv_ref[2]
    scale = HEAD ** (-0.5)
    grads = [[], [], []]
    for head in range(queries.shape[1] // HEAD):
        lanes = slice(head * HEAD, (head + 1) * HEAD)
        query, key, value = queries[:, lanes], keys_low[:, lanes], values_low[:, lanes]
        outer = context_grad[:, lanes]
        weights = softmax_rows(dot_nt(query, key) * scale)
        prob_dot = dot_nt(outer, value)
        score_grad = (
            weights * (prob_dot - jnp.sum(weights * prob_dot, axis=1, keepdims=True))
        ).astype(BF)
        grads[0].append(dot(score_grad, key) * scale)
        grads[1].append(dot_tn(score_grad, query) * scale)
        grads[2].append(dot_tn(weights.astype(BF), outer))
    partial = None
    sums = []
    for i in range(3):
        grad = jnp.concatenate(grads[i], axis=1).astype(BF)
        dqkv_ref[i] = grad
        sums.append(jnp.sum(grad.astype(F32), axis=0, keepdims=True))
        part = dot(grad, weight_ref[0, i])
        partial = part if partial is None else partial + part
    unit_one, inverse_one = normalized(hidden_ref[...].astype(F32))
    width = partial.shape[1]
    rows_ref[...] = jnp.zeros_like(rows_ref)
    rows_ref[0:1] = jnp.sum(second_grad * unit_two, axis=0, keepdims=True)
    rows_ref[1:2] = jnp.sum(second_grad, axis=0, keepdims=True)
    rows_ref[2:3] = jnp.sum(dh, axis=0, keepdims=True)
    rows_ref[3:4] = jnp.concatenate(
        [sums[0], sums[2], jnp.zeros((1, width - 2 * share), F32)], axis=1
    )
    rows_ref[4:5] = jnp.sum(partial * unit_one, axis=0, keepdims=True)
    rows_ref[5:6] = jnp.sum(partial, axis=0, keepdims=True)

    def spread_rows(values):
        padded[...] = jnp.zeros_like(padded)
        padded[0:tokens] = values

    def rows_of(step):
        start = pl.multiple_of(lax.rem(me + step, count) * block, 8)
        return padded[pl.ds(start, block)]

    spread_rows(partial)
    for step in range(count):
        block_refs[step][...] = rows_of(step).astype(BF)
    spread_rows(unit_one)
    unit_ref[...] = rows_of(0)
    spread_rows(jnp.broadcast_to(inverse_one, partial.shape))
    inverse_ref[...] = rows_of(0)[:, 0:128]


def norm_rows_kernel(layer, p0, p1, p2, p3, unit_ref, inverse_ref, gain_ref, out_ref):
    total = p0[...].astype(F32) + p1[...].astype(F32) + p2[...].astype(F32) + p3[...].astype(F32)
    out_ref[...] = norm_backward(
        total, unit_ref[...], inverse_ref[:, 0:1], row_of(gain_ref, layer, 0)
    ).astype(BF)


def pack_kernel(first_ref, dqkv_ref, context_ref, dz_ref, second_ref, dlogit_ref, rows_ref, core_ref, mine_ref, away_ref, target):
    width = first_ref.shape[1]
    share = dqkv_ref.shape[2]
    experts = dlogit_ref.shape[1]
    half = (width + experts) // 2
    size = target.shape[0] // 2
    gap = size - half

    def put(start, values):
        stop = start + values.shape[0]
        if stop <= half:
            target[start:stop] = values
        elif start >= half:
            target[start + gap : stop + gap] = values
        else:
            target[start:half] = values[: half - start]
            target[size : stop + gap] = values[half - start :]

    first_low = first_ref[...]
    for i in range(3):
        put(i * share, dot_tn(dqkv_ref[i], first_low))
    put(3 * share, dot_tn(context_ref[...], dz_ref[...]))
    put(width, dot_tn(dlogit_ref[...], second_ref[...]))
    small = jnp.concatenate([rows_ref[...], jnp.zeros((gap - 8, width), F32)], axis=0)
    target[half:size] = small
    target[size + half :] = small
    core = core_ref[0]
    mine_ref[...] = target[pl.ds(pl.multiple_of(core * size, 8), size)].astype(BF)
    away_ref[...] = target[pl.ds(pl.multiple_of((1 - core) * size, 8), size)].astype(BF)


def sum_kernel(count, pieces, index_ref, *rest):
    parts, outs, scratch = rest[:count], rest[count : count + pieces], rest[-1]
    total = parts[0][...].astype(F32)
    for part in parts[1:]:
        total = total + part[...].astype(F32)
    if pieces == 1:
        outs[0][...] = total.astype(BF)
        return
    rows = outs[0].shape[0]
    scratch[0 : total.shape[0]] = total
    if scratch.shape[0] > total.shape[0]:
        scratch[total.shape[0] :] = jnp.zeros(
            (scratch.shape[0] - total.shape[0], total.shape[1]), F32
        )
    for step in range(pieces):
        start = pl.multiple_of(lax.rem(index_ref[0] + step, pieces) * rows, 8)
        outs[step][...] = scratch[pl.ds(start, rows)].astype(BF)


def ordered_sum_kernel(count, index_ref, *rest):
    parts, out_ref, scratch = rest[:count], rest[count], rest[count + 1]
    for step in range(count):
        scratch[step] = parts[step][...].astype(F32)
    total = scratch[in_order(index_ref[0], 0, count)]
    for j in range(1, count):
        total = total + scratch[in_order(index_ref[0], j, count)]
    out_ref[...] = total.astype(BF)


def order_kernel(count, index_ref, *rest):
    parts, out_ref, scratch = rest[:count], rest[count], rest[count + 1]
    rows = parts[0].shape[0]
    for step in range(count):
        start = pl.multiple_of(in_order(index_ref[0], step, count) * rows, 8)
        scratch[pl.ds(start, rows)] = parts[step][...].astype(F32)
    out_ref[...] = scratch[0 : out_ref.shape[0]].astype(BF)


def add_rows_kernel(count, me_ref, base_ref, *rest):
    parts, out_ref, scratch = rest[:count], rest[count], rest[count + 1]
    rows = parts[0].shape[0]
    for step in range(count):
        start = pl.multiple_of(in_order(me_ref[0], step, count) * rows, 8)
        scratch[pl.ds(start, rows)] = parts[step][...].astype(F32)
    out_ref[...] = base_ref[...] + scratch[0 : out_ref.shape[0]]


def add_columns_kernel(count, me_ref, base_ref, *rest):
    parts, out_ref, scratch = rest[:count], rest[count], rest[count + 1]
    for step in range(count):
        scratch[step] = parts[step][...]
    out_ref[...] = base_ref[...] + joined_columns(scratch, me_ref[0], count, out_ref.shape[0])


def unpack_kernel(core_ref, me_ref, *rest):
    levels, smalls, outs = rest[:4], rest[4:8], rest[8:12]
    scratch, small_scratch = rest[12:]
    inw_ref, outw_ref, route_ref, rows_ref = outs
    size = levels[0].shape[0]
    core = core_ref[0]
    share, width = inw_ref.shape[2], inw_ref.shape[3]
    experts = route_ref.shape[1]
    half = (width + experts) // 2
    gap = size - half
    count = len(smalls)
    for step in range(count):
        small_scratch[step] = smalls[step][...].astype(F32)
    small = small_scratch[in_order(me_ref[0], 0, count)]
    for j in range(1, count):
        small = small + small_scratch[in_order(me_ref[0], j, count)]
    for layer in range(2):
        mine_ref, other_ref = levels[2 * layer], levels[2 * layer + 1]
        scratch[pl.ds(pl.multiple_of(core * size, 8), size)] = mine_ref[...].astype(F32)
        scratch[pl.ds(pl.multiple_of((1 - core) * size, 8), size)] = other_ref[...].astype(F32)

        def rows(start, stop):
            if stop <= half:
                return scratch[start:stop]
            if start >= half:
                return scratch[start + gap : stop + gap]
            return jnp.concatenate([scratch[start:half], scratch[size : stop + gap]], axis=0)

        for i in range(3):
            inw_ref[layer, i] = rows(i * share, (i + 1) * share)
        outw_ref[layer] = rows(3 * share, width)
        route_ref[layer] = rows(width, width + experts)
        rows_ref[layer, 0:4] = scratch[half : half + 4]
        rows_ref[layer, 4:8] = small[8 * layer + 4 : 8 * layer + 8]


def write_chunks(total, out_ref, part_index=0):
    devices, _, half, _ = out_ref.shape
    rows = total.reshape(devices, 2 * half, total.shape[1])
    lower, upper = rows[:, :half], rows[:, half:]
    tile = total.shape[1] // 6
    part = tile // 2
    for j in range(4):
        first = slice(j * tile, (j + 1) * tile)
        rest = slice(4 * tile + j * part, 4 * tile + (j + 1) * part)
        mixed = jnp.concatenate([lower[:, :, rest], upper[:, :, rest]], axis=2)
        block = jnp.concatenate([lower[:, :, first], upper[:, :, first], mixed], axis=2)
        lanes = slice(part_index * 3 * tile, (part_index + 1) * 3 * tile)
        out_ref[:, j, :, lanes] = block.astype(BF)


def forward_kernel(layer, me_ref, x_ref, up_ref, up_bias_ref, down_ref, down_bias_ref, chunk_ref, active_ref, slope_ref, total):
    step = pl.program_id(0)
    rows = x_ref[...].reshape(total.shape)
    pre = jnp.dot(rows, up_ref[0, 0], preferred_element_type=F32)
    pre = pre + up_bias_ref[...].astype(F32)[0, layer : layer + 1]
    half_cdf = 0.5 * (1.0 + lax.erf(pre * 0.7071067811865476))
    active = (pre * half_cdf).astype(BF)
    active_ref[...] = active
    slope_ref[...] = half_cdf + pre * jnp.exp(-0.5 * pre * pre) * 0.3989422804014327
    part = jnp.dot(active, down_ref[0, 0], preferred_element_type=F32)

    @pl.when(step == 0)
    def _():
        offset = down_bias_ref[...].astype(F32)[0, layer : layer + 1]
        total[...] = part + jnp.where(me_ref[0] == 0, offset, 0.0)

    @pl.when(step > 0)
    def _():
        total[...] += part

    @pl.when(step == pl.num_programs(0) - 1)
    def _():
        write_chunks(total[...], chunk_ref)


def backward_kernel(dy_ref, slope_ref, up_ref, down_ref, chunk_ref, pre_grad_ref, total):
    step = pl.program_id(0)
    out_grad = dy_ref[...].reshape(total.shape)
    pre_grad = (dot_nt(out_grad, down_ref[0, 0]) * slope_ref[...]).astype(BF)
    pre_grad_ref[...] = pre_grad
    part = dot_nt(pre_grad, up_ref[0, 0])

    @pl.when(step == 0)
    def _():
        total[...] = part

    @pl.when(step > 0)
    def _():
        total[...] += part

    @pl.when(step == pl.num_programs(0) - 1)
    def _():
        write_chunks(total[...], chunk_ref)


def both_kernel(
    layer,
    me_ref,
    x_ref,
    grad_ref,
    up_ref,
    up_bias_ref,
    down_ref,
    down_bias_ref,
    chunk_ref,
    active_ref,
    pre_grad_ref,
    dy_ref,
    out_total,
    back_total,
):
    step = pl.program_id(0)
    rows, width = out_total.shape

    @pl.when(step == 0)
    def _():
        gate = jnp.sum(x_ref[:, :, width:].astype(F32).reshape(rows, -1), axis=1, keepdims=True)
        dy_ref[...] = (gate * grad_ref[...].reshape(rows, width).astype(F32)).astype(BF).reshape(
            dy_ref.shape
        )
        offset = down_bias_ref[...].astype(F32)[0, layer : layer + 1]
        offset = jnp.where(me_ref[0] == 0, offset, 0.0)
        out_total[...] = jnp.broadcast_to(offset, out_total.shape)
        back_total[...] = jnp.zeros_like(back_total)

    arrived = x_ref[:, :, :width].reshape(rows, width)
    pre = dot(arrived, up_ref[0, 0]) + up_bias_ref[...].astype(F32)[0, layer : layer + 1]
    half_cdf = 0.5 * (1.0 + lax.erf(pre * 0.7071067811865476))
    active = (pre * half_cdf).astype(BF)
    active_ref[...] = active
    slope = half_cdf + pre * jnp.exp(-0.5 * pre * pre) * 0.3989422804014327
    out_total[...] += dot(active, down_ref[0, 0])
    pre_grad = (dot_nt(dy_ref[...].reshape(rows, width), down_ref[0, 0]) * slope).astype(BF)
    pre_grad_ref[...] = pre_grad
    back_total[...] += dot_nt(pre_grad, up_ref[0, 0])

    @pl.when(step == pl.num_programs(0) - 1)
    def _():
        write_chunks(out_total[...], chunk_ref, 0)
        write_chunks(back_total[...], chunk_ref, 1)


def weight_kernel(x_ref, dy_ref, active_ref, pre_grad_ref, *rest):
    up_ref, up_bias_ref, down_ref, down_bias_ref = rest[-4:]
    shape = active_ref.shape[0], dy_ref.shape[2]
    pre_grad = pre_grad_ref[...]
    out_grad = dy_ref[...].reshape(shape)
    up_ref[0, 0] = dot_tn(x_ref[...].reshape(shape), pre_grad)
    down_ref[0, 0] = dot_tn(active_ref[...], out_grad)
    up_bias_ref[0] = jnp.sum(pre_grad.astype(F32), axis=0, keepdims=True)

    @pl.when(pl.program_id(0) == 0)
    def _():
        down_bias_ref[0] = jnp.sum(out_grad.astype(F32), axis=0, keepdims=True)


FBLOCK = 256
PARAMS = dict(vmem_limit_bytes=48 * 1024 * 1024)


def smem():
    return pl.BlockSpec(memory_space=pltpu.SMEM)


def near_out(shape, kind):
    return jax.ShapeDtypeStruct(shape, kind)


def far_out(shape, kind):
    return pltpu.HBM(shape, kind)


def far(value):
    return pltpu.with_memory_space_constraint(value, pltpu.HBM)


def call(kernel, name, outs, operands, scratch=(), specs=None):
    specs = specs or {}
    in_specs = [
        specs.get(i, smem() if operand.shape == (1,) else whole(operand.shape))
        for i, operand in enumerate(operands)
    ]
    return pl.pallas_call(
        kernel,
        grid=(1,),
        in_specs=in_specs,
        out_specs=[whole(out.shape) for out in outs],
        out_shape=outs,
        scratch_shapes=[pltpu.VMEM(shape, kind) for shape, kind in scratch],
        compiler_params=pltpu.CompilerParams(**PARAMS),
        name=name,
    )(*operands)


def layer_block(array, layer):
    shape = (1,) + array.shape[1:]
    return pl.BlockSpec(shape, lambda step: (layer,) + (0,) * (len(shape) - 1))


def whole(shape):
    return pl.BlockSpec(shape, lambda step: (0,) * len(shape))


def expert_forward(layer, me_one, arrived, up_weight, up_bias, down_weight, down_bias):
    devices, slots, width = arrived.shape
    hidden = up_weight.shape[3]
    rows = devices * slots
    return pl.pallas_call(
        functools.partial(forward_kernel, layer),
        grid=(hidden // FBLOCK,),
        in_specs=[
            smem(),
            whole(arrived.shape),
            pl.BlockSpec((1, 1, width, FBLOCK), lambda step: (layer, 0, 0, step)),
            pl.BlockSpec((1, up_bias.shape[1], FBLOCK), lambda step: (0, 0, step)),
            pl.BlockSpec((1, 1, FBLOCK, width), lambda step: (layer, 0, step, 0)),
            whole(down_bias.shape),
        ],
        out_specs=[
            whole((devices, 4, slots // 2, width // 2)),
            pl.BlockSpec((rows, FBLOCK), lambda step: (0, step)),
            pl.BlockSpec((rows, FBLOCK), lambda step: (0, step)),
        ],
        out_shape=[
            jax.ShapeDtypeStruct((devices, 4, slots // 2, width // 2), BF),
            pltpu.HBM((rows, hidden), BF),
            pltpu.HBM((rows, hidden), F32),
        ],
        scratch_shapes=[pltpu.VMEM((rows, width), F32)],
        compiler_params=pltpu.CompilerParams(**PARAMS),
        name="expert_forward",
    )(me_one, arrived, *map(far, (up_weight, up_bias, down_weight, down_bias)))


def expert_backward(layer, out_grad, slope, up_weight, down_weight):
    devices, slots, width = out_grad.shape
    hidden = up_weight.shape[3]
    rows = devices * slots
    chunk = (devices, 4, slots // 2, width // 2)
    return pl.pallas_call(
        backward_kernel,
        grid=(hidden // FBLOCK,),
        in_specs=[
            whole(out_grad.shape),
            pl.BlockSpec((rows, FBLOCK), lambda step: (0, step)),
            pl.BlockSpec((1, 1, width, FBLOCK), lambda step: (layer, 0, 0, step)),
            pl.BlockSpec((1, 1, FBLOCK, width), lambda step: (layer, 0, step, 0)),
        ],
        out_specs=[whole(chunk), pl.BlockSpec((rows, FBLOCK), lambda step: (0, step))],
        out_shape=[jax.ShapeDtypeStruct(chunk, BF), pltpu.HBM((rows, hidden), BF)],
        scratch_shapes=[pltpu.VMEM((rows, width), F32)],
        compiler_params=pltpu.CompilerParams(**PARAMS),
        name="expert_backward",
    )(out_grad, *map(far, (slope, up_weight, down_weight)))


def expert_both(layer, me_one, arrived, grad_rows, up_weight, up_bias, down_weight, down_bias):
    devices, slots, width = grad_rows.shape
    hidden = up_weight.shape[3]
    rows = devices * slots
    chunk = (devices, 4, slots // 2, width)
    return pl.pallas_call(
        functools.partial(both_kernel, layer),
        grid=(hidden // FBLOCK,),
        in_specs=[
            smem(),
            whole(arrived.shape),
            whole(grad_rows.shape),
            pl.BlockSpec((1, 1, width, FBLOCK), lambda step: (layer, 0, 0, step)),
            pl.BlockSpec((1, up_bias.shape[1], FBLOCK), lambda step: (0, 0, step)),
            pl.BlockSpec((1, 1, FBLOCK, width), lambda step: (layer, 0, step, 0)),
            whole(down_bias.shape),
        ],
        out_specs=[
            whole(chunk),
            pl.BlockSpec((rows, FBLOCK), lambda step: (0, step)),
            pl.BlockSpec((rows, FBLOCK), lambda step: (0, step)),
            whole(grad_rows.shape),
        ],
        out_shape=[
            jax.ShapeDtypeStruct(chunk, BF),
            pltpu.HBM((rows, hidden), BF),
            pltpu.HBM((rows, hidden), BF),
            pltpu.HBM(grad_rows.shape, BF),
        ],
        scratch_shapes=[pltpu.VMEM((rows, width), F32), pltpu.VMEM((rows, width), F32)],
        compiler_params=pltpu.CompilerParams(**PARAMS),
        name="expert_both",
    )(me_one, arrived, *map(far, (grad_rows, up_weight, up_bias, down_weight, down_bias)))


def expert_weights(layer, layers, arrived, out_grad, active, pre_grad, earlier):
    devices, slots, width = out_grad.shape
    rows, hidden = active.shape
    operands = [*map(far, (arrived, out_grad, active, pre_grad))] + list(earlier or ())
    return pl.pallas_call(
        weight_kernel,
        grid=(hidden // FBLOCK,),
        in_specs=[
            whole(out_grad.shape),
            whole(out_grad.shape),
            pl.BlockSpec((rows, FBLOCK), lambda step: (0, step)),
            pl.BlockSpec((rows, FBLOCK), lambda step: (0, step)),
        ]
        + [pl.BlockSpec(memory_space=pl.ANY)] * len(earlier or ()),
        out_specs=[
            pl.BlockSpec((1, 1, width, FBLOCK), lambda step: (layer, 0, 0, step)),
            pl.BlockSpec((1, 1, FBLOCK), lambda step: (layer, 0, step)),
            pl.BlockSpec((1, 1, FBLOCK, width), lambda step: (layer, 0, step, 0)),
            pl.BlockSpec((1, 1, width), lambda step: (layer, 0, 0)),
        ],
        out_shape=[
            pltpu.HBM((layers, 1, width, hidden), F32),
            pltpu.HBM((layers, 1, hidden), F32),
            pltpu.HBM((layers, 1, hidden, width), F32),
            pltpu.HBM((layers, 1, width), F32),
        ],
        input_output_aliases={4 + i: i for i in range(len(earlier or ()))},
        compiler_params=pltpu.CompilerParams(**PARAMS),
        name="expert_weights",
    )(*operands)


def cycle(size, step):
    return [(place, (place + step) % size) for place in range(size)]


def body(
    tokens,
    expert_ids,
    norm_gain,
    norm_bias,
    input_weight,
    input_bias,
    output_weight,
    output_bias,
    router_weight,
    up_weight,
    up_bias,
    down_weight,
    down_bias,
    cotangent,
):
    token_count, width = tokens.shape
    layer_count = norm_gain.shape[0]
    share = input_weight.shape[3]
    experts = router_weight.shape[2]
    devices = lax.axis_size("expert")
    shards = lax.axis_size("shard")
    capacity = 5 * token_count // (2 * experts) + 1
    slots = experts * capacity
    me = lax.axis_index("shard")
    place = lax.axis_index("expert")
    me_one = me.reshape(1)
    row_block = 8 * (-(-token_count // (8 * shards)))
    size = 32 * (-(-((width + experts) // 2 + 8) // 32))

    cores = 2
    side = 4
    core, z_place, x_place = place % cores, (place // cores) % side, place // (cores * side)
    core_one, z_one, x_one = core.reshape(1), z_place.reshape(1), x_place.reshape(1)

    def core_pairs():
        return [(p, p ^ 1) for p in range(devices)]

    def z_pairs(step):
        return [(p, (p // 8) * 8 + ((p // 2 + step) % 4) * 2 + p % 2) for p in range(devices)]

    def x_pairs(step):
        return [(p, ((p // 8 + step) % 4) * 8 + p % 8) for p in range(devices)]

    def spread(value):
        return [value] + [
            lax.ppermute(value, "shard", cycle(shards, step)) for step in range(1, shards)
        ]

    def exchange(blocks):
        return [blocks[0]] + [
            lax.ppermute(blocks[step], "shard", cycle(shards, step)) for step in range(1, shards)
        ]

    def to_owners(rows):
        outgoing = rows.reshape(devices, capacity, rows.shape[1])
        return lax.all_to_all(outgoing, "expert", split_axis=0, concat_axis=0, tiled=True)

    def go_back(chunks):
        flat = chunks.reshape(-1, *chunks.shape[2:])
        back = lax.all_to_all(
            flat, ("expert", "shard"), split_axis=0, concat_axis=0, tiled=True
        )
        return back.reshape(chunks.shape)

    gains, shifts = far(norm_gain), far(norm_bias)
    in_bias, out_bias = far(input_bias), far(output_bias)
    up_rows, down_rows = jnp.swapaxes(up_bias, 0, 1), jnp.swapaxes(down_bias, 0, 1)
    ids = far(expert_ids)
    pair = (token_count, 2)
    square = (token_count, width)
    narrow = (token_count, share)
    fold_rows = 8 * (-(-token_count // 16))
    fold = (fold_rows, 2 * share)
    fold_more = (fold_rows + 8, 2 * share)
    in_weight = far(jnp.swapaxes(input_weight, 2, 3))
    router = far(jnp.swapaxes(router_weight, 1, 2))
    out_weight = far(output_weight)

    def attention_forward(layer, base, parts):
        joins = len(parts)
        operands = [me_one, base, *parts, gains, shifts, in_weight, in_bias]
        outs = [
            far_out(square, BF),
            far_out((3,) + narrow, BF),
            far_out(narrow, BF),
            near_out(fold, BF),
        ]
        scratch = []
        if joins:
            outs.append(far_out(square, F32))
            scratch.append(((joins,) + fold, BF))
        found = call(
            functools.partial(attention_kernel, layer, joins),
            "attention_forward",
            outs,
            operands,
            scratch,
            specs={joins + 4: layer_block(in_weight, layer)},
        )
        return found if joins else [*found, base]

    def weight_pieces(weight):
        rows = weight.shape[0] // cores
        near = spread(lax.dynamic_slice_in_dim(weight, core * rows, rows, 0))[1:]
        return near + [to_core(value) for value in near]

    def route(layer, hidden, context_fold, pieces, more=0):
        return call(
            functools.partial(route_kernel, layer, capacity),
            "route",
            [
                far_out(square, F32),
                far_out(square, BF),
                far_out((token_count, experts), F32),
                far_out(pair, F32),
                far_out(pair, jnp.int32),
                near_out((slots, width + more), BF),
            ],
            [
                me_one,
                core_one,
                far(hidden),
                *context_fold,
                out_weight,
                *pieces,
                out_bias,
                gains,
                shifts,
                router,
                ids,
            ],
            [((shards,) + fold, BF), ((shards, share, width), BF)],
            specs={7: layer_block(out_weight, layer)},
        )

    def send_grads(base, parts, gate_values, columns):
        joins = len(parts)
        outs = [near_out((slots, width), BF)]
        scratch = []
        if joins:
            outs.append(far_out(square, F32))
            scratch.append(((joins * row_block, width), F32))
        return call(
            functools.partial(send_kernel, joins),
            "send_grads",
            outs,
            [me_one, base, *parts, far(gate_values), far(columns)],
            scratch,
        )

    def combine(arrived, gate_values, columns, incoming=None, kept=None):
        has_back, has_out = incoming is not None, kept is None
        outs = []
        if has_out:
            outs.append((far_out if has_back else near_out)(fold, BF))
            if not has_back:
                outs.append(far_out((2,) + narrow, BF))
        if has_back:
            outs.append(near_out(fold_more, BF))
        operands = [me_one, arrived, far(gate_values), far(columns)]
        operands += [far(value) for value in (incoming, kept) if value is not None]
        return call(
            functools.partial(combine_kernel, has_out, has_back, capacity),
            "combine",
            outs,
            operands,
        )

    def run_forward(layer, arrived):
        return expert_forward(layer, me_one, arrived, up_weight, up_rows, down_weight, down_rows)

    def block_backward(layer, incoming, parts, middle, hidden, prob, gate_values, qkv):
        block = near_out((row_block, width), BF)
        out = near_out if layer == 0 else far_out
        return call(
            functools.partial(backward_block_kernel, layer, share, row_block),
            "backward_block",
            [
                (far_out if layer == 0 else near_out)(square, F32),
                out((3,) + narrow, BF),
                out(square, BF),
                out((token_count, experts), BF),
                out((8, width), F32),
                block,
                block,
                block,
                block,
                near_out((row_block, width), F32),
                near_out((row_block, 128), F32),
            ],
            [
                me_one,
                far(incoming),
                *parts,
                far(middle),
                far(hidden),
                far(prob),
                far(gate_values),
                ids,
                far(qkv),
                gains,
                router,
                out_weight,
                in_weight,
            ],
            [((shards,) + fold_more, BF), ((shards * row_block, width), F32)],
            specs={
                14: layer_block(output_weight, layer),
                15: layer_block(in_weight, layer),
            },
        )

    def norm_rows(layer, blocks, unit, inverse):
        return call(
            functools.partial(norm_rows_kernel, layer),
            "norm_rows",
            [near_out((row_block, width), BF)],
            [*blocks, unit, inverse, gains],
        )[0]

    def pack(first_low, dqkv, context, dz, second_low, dlogit, rows):
        half = near_out((size, width), BF)
        return call(
            pack_kernel,
            "pack",
            [half, half],
            [first_low, dqkv, context, dz, second_low, dlogit, rows, core_one],
            [((2 * size, width), F32)],
        )

    quarter = size // side

    def sums(parts, index, pieces, rows):
        return call(
            functools.partial(sum_kernel, len(parts), pieces),
            "sums",
            [near_out((rows, width), BF)] * pieces,
            [index, *parts],
            [((pieces * rows, width), F32)],
        )

    def ordered_sum(parts, index):
        shape = parts[0].shape
        return call(
            functools.partial(ordered_sum_kernel, len(parts)),
            "ordered_sum",
            [near_out(shape, BF)],
            [index, *parts],
            [((len(parts),) + shape, F32)],
        )[0]

    def ordered(parts, index, rows):
        return call(
            functools.partial(order_kernel, len(parts)),
            "ordered",
            [near_out((rows, width), BF)],
            [index, *parts],
            [((len(parts) * parts[0].shape[0], width), F32)],
        )[0]

    def sent(blocks, pairs):
        return [blocks[0]] + [
            lax.ppermute(blocks[step], "expert", pairs(step)) for step in range(1, side)
        ]

    def to_core(value):
        return lax.ppermute(value, "expert", core_pairs())

    def tied(*values):
        return lax.optimization_barrier(values)

    pieces = weight_pieces(output_weight[0])
    first0, qkv0, context0, fold0, hidden0 = attention_forward(0, tokens, [])
    middle0, second0, prob0, gate0, column0, send = route(0, hidden0, spread(fold0), pieces)
    send, later_weight = tied(send, output_weight[1])
    arrived0 = to_owners(send)
    arrived0, *pieces = tied(arrived0, *weight_pieces(later_weight))
    chunks, active0, slope0 = run_forward(0, arrived0)
    back = go_back(chunks)
    mixed, kept0 = combine(back, gate0, column0)

    mixed_parts = spread(mixed)
    (send_rows,) = call(
        functools.partial(early_kernel, 1, capacity, experts),
        "early_rows",
        [far_out((slots, width), BF)],
        [ids, far(cotangent)],
    )
    send_rows, mixed_parts[0] = tied(send_rows, mixed_parts[0])
    first1, qkv1, context1, fold1, hidden1 = attention_forward(1, far(middle0), mixed_parts)
    grad_rows = to_owners(send_rows)
    grad_rows, *fold1 = tied(grad_rows, *spread(fold1))
    middle1, second1, prob1, gate1, column1, send = route(1, hidden1, fold1, pieces, 128)
    arrived1 = to_owners(send)
    chunks, active1, pre_grad1, out_grad1 = expert_both(
        1, me_one, arrived1, grad_rows, up_weight, up_rows, down_weight, down_rows
    )
    back = go_back(chunks)
    expert_grads = expert_weights(
        1, layer_count, arrived1, out_grad1, active1, pre_grad1, None
    )
    back, *expert_grads = tied(back, *expert_grads)
    mixed, shares = combine(back, gate1, column1, incoming=cotangent)

    dh1, dqkv1, dz1, dlogit1, rows1, *blocks, unit, inverse = block_backward(
        1, cotangent, spread(shares), middle1, hidden1, prob1, gate1, qkv1
    )
    parts = spread(norm_rows(1, exchange(blocks), unit, inverse))
    send, incoming = send_grads(dh1, parts, gate0, column0)

    out_grad0 = to_owners(send)
    mine1, away1 = pack(*map(far, (first1, dqkv1, context1, dz1, second1, dlogit1, rows1)))
    away1 = to_core(away1)
    level1 = sent(sums([mine1, away1], x_one, side, quarter), x_pairs)
    out_grad0, *level1 = tied(out_grad0, *level1)
    back_chunks, pre_grad0 = expert_backward(0, out_grad0, slope0, up_weight, down_weight)
    back = go_back(back_chunks)
    expert_grads = expert_weights(
        0, layer_count, arrived0, out_grad0, active0, pre_grad0, expert_grads
    )
    mixed = spread(mixed)
    output = call(
        functools.partial(add_columns_kernel, shards),
        "add_columns",
        [far_out(square, F32)],
        [me_one, far(middle1), *mixed],
        [((shards,) + fold, BF)],
    )[0]
    level1 = sent(sums(level1, x_one, 1, quarter) * side, z_pairs)
    back, output, *level1 = tied(back, output, *level1)
    (shares,) = combine(back, gate0, column0, incoming=incoming, kept=kept0)
    shares = spread(shares)
    dh0, dqkv0, dz0, dlogit0, rows0, *blocks, unit, inverse = block_backward(
        0, incoming, shares, middle0, hidden0, prob0, gate0, qkv0
    )
    level1 = sent([ordered_sum(level1, z_one)] * side, x_pairs)
    dqkv0, *level1 = tied(dqkv0, *level1)
    mine, away = pack(
        far(first0), dqkv0, far(context0), dz0, far(second0), dlogit0, rows0
    )
    away = to_core(away)

    level1 = ordered(level1, x_one, size)
    other1 = to_core(level1)
    away, other1 = tied(away, other1)
    blocks = exchange(blocks)
    level = sent(sums([mine, away], z_one, side, quarter), z_pairs)
    rest = tied(*level, *blocks)
    level, blocks = rest[:side], rest[side:]
    level = sent(sums(level, z_one, 1, quarter) * side, x_pairs)
    parts = spread(norm_rows(0, blocks, unit, inverse))
    rest = tied(*level, *parts)
    level, parts = rest[:side], rest[side:]
    level = sent([ordered_sum(level, x_one)] * side, z_pairs)
    rest = tied(*level, *expert_grads)
    level, expert_grads = rest[:side], rest[side:]
    level = ordered(level, z_one, size)
    other = to_core(level)
    half = (width + experts) // 2
    small = spread(jnp.concatenate([level[half : half + 8], level1[half : half + 8]], axis=0))
    grad_tokens = call(
        functools.partial(add_rows_kernel, shards),
        "add_rows",
        [far_out(square, F32)],
        [me_one, far(dh0), *parts],
        [((shards * row_block, width), F32)],
    )[0]
    inw, outw, router_grad, rows = call(
        unpack_kernel,
        "unpack",
        [
            far_out((layer_count, 3, share, width), F32),
            far_out((layer_count, share, width), F32),
            far_out((layer_count, experts, width), F32),
            near_out((layer_count, 8, width), F32),
        ],
        [core_one, me_one, level, other, level1, other1, *small],
        [((2 * size, width), F32), ((shards, 16, width), F32)],
    )
    return (
        output,
        grad_tokens,
        jnp.stack([rows[:, 4], rows[:, 0]], axis=1),
        jnp.stack([rows[:, 5], rows[:, 1]], axis=1),
        jnp.swapaxes(inw, 2, 3),
        rows[:, 3, : 2 * share].reshape(layer_count, 2, share),
        outw,
        rows[:, 2],
        jnp.swapaxes(router_grad, 1, 2),
        *expert_grads,
    )


def solution(mesh):
    return jax.shard_map(
        body,
        mesh=mesh,
        in_specs=(
            P("expert", None),
            P(None, "expert", None),
            P(),
            P(),
            P(None, None, None, "shard"),
            P(None, None, "shard"),
            P(None, "shard", None),
            P(),
            P(),
            P(None, "expert", None, "shard"),
            P(None, "expert", "shard"),
            P(None, "expert", "shard", None),
            P(None, "expert", None),
            P("expert", None),
        ),
        out_specs=(
            P("expert", None),
            P("expert", None),
            P(),
            P(),
            P(None, None, None, "shard"),
            P(None, None, "shard"),
            P(None, "shard", None),
            P(),
            P(),
            P(None, "expert", None, "shard"),
            P(None, "expert", "shard"),
            P(None, "expert", "shard", None),
            P(None, "expert", None),
        ),
        check_vma=False,
    )
```

```python
import functools

import jax
import jax.numpy as jnp
from jax import lax
from jax.experimental import pallas as pl
from jax.experimental.pallas import tpu as pltpu
from jax.sharding import PartitionSpec as P

HEAD = 64
BF = jnp.bfloat16
F32 = jnp.float32

eps = 1e-06


def dot(left, right):
    return jnp.dot(left, right, preferred_element_type=F32)


def dot_nt(left, right):
    return lax.dot_general(left, right, (((1,), (1,)), ((), ())), preferred_element_type=F32)


def dot_tn(left, right):
    return lax.dot_general(left, right, (((0,), (0,)), ((), ())), preferred_element_type=F32)


def normalized(values):
    centred = values - jnp.mean(values, axis=1, keepdims=True)
    inverse = lax.rsqrt(jnp.mean(centred * centred, axis=1, keepdims=True) + eps)
    return centred * inverse, inverse


def norm_backward(incoming, normed, inverse, gain_row):
    scaled = incoming * gain_row
    return inverse * (
        scaled
        - jnp.mean(scaled, axis=1, keepdims=True)
        - normed * jnp.mean(scaled * normed, axis=1, keepdims=True)
    )


def softmax_rows(scores):
    raised = jnp.exp(scores - jnp.max(scores, axis=1, keepdims=True))
    return raised / jnp.sum(raised, axis=1, keepdims=True)


def one_hot(column, size):
    places = lax.broadcasted_iota(jnp.int32, (column.shape[0], size), 1)
    return places == column


def low(mask):
    return mask.astype(F32).astype(BF)


def row_of(ref, layer, row):
    return ref[...].astype(F32)[layer][row : row + 1]


def in_order(me, place, count):
    return lax.rem(me + count - place, count)


def folded(values, extra=None):
    rows, lanes = values.shape
    half = 8 * (-(-rows // 16))
    padding = jnp.zeros((2 * half - rows, lanes), F32)
    values = jnp.concatenate([values.astype(F32), padding], axis=0)
    sides = [jnp.concatenate([values[:half], values[half:]], axis=1)]
    if extra is not None:
        sides.append(extra)
    return jnp.concatenate(sides, axis=0).astype(BF)


def unfolded(values, rows):
    half, lanes = 8 * (-(-rows // 16)), values.shape[1] // 2
    values = values[:half]
    return jnp.concatenate([values[:, :lanes], values[:, lanes:]], axis=0)[:rows]


def joined_columns(parts_ref, me, count, rows):
    parts = [
        unfolded(parts_ref[in_order(me, j, count)].astype(F32), rows) for j in range(count)
    ]
    share = parts[0].shape[1]
    tile = 2 * share // 3
    return jnp.concatenate(
        [part[:, :tile] for part in parts] + [part[:, tile:] for part in parts], axis=1
    )


def attention_kernel(layer, joins, me_ref, hidden_ref, *rest):
    parts, rest = rest[:joins], rest[joins:]
    gain_ref, shift_ref, weight_ref, bias_ref, first_ref, qkv_ref, context_ref, fold_ref = rest[:8]
    hidden = hidden_ref[...].astype(F32)
    if joins:
        hidden_out, scratch = rest[8:]
        for step in range(joins):
            scratch[step] = parts[step][...]
        hidden = hidden + joined_columns(scratch, me_ref[0], joins, hidden.shape[0])
        hidden_out[...] = hidden
    unit, _ = normalized(hidden)
    first_low = (unit * row_of(gain_ref, layer, 0) + row_of(shift_ref, layer, 0)).astype(BF)
    first_ref[...] = first_low
    bias = bias_ref[...].astype(F32)[layer]
    queries = (dot_nt(first_low, weight_ref[0, 0]) + bias[0:1]).astype(BF)
    keys_low = dot_nt(first_low, weight_ref[0, 1]).astype(BF)
    values_low = (dot_nt(first_low, weight_ref[0, 2]) + bias[1:2]).astype(BF)
    qkv_ref[0] = queries
    qkv_ref[1] = keys_low
    qkv_ref[2] = values_low
    contexts = []
    for head in range(queries.shape[1] // HEAD):
        lanes = slice(head * HEAD, (head + 1) * HEAD)
        scores = dot_nt(queries[:, lanes], keys_low[:, lanes]) * (HEAD ** (-0.5))
        contexts.append(dot(softmax_rows(scores).astype(BF), values_low[:, lanes]))
    context = jnp.concatenate(contexts, axis=1).astype(BF)
    context_ref[...] = context
    fold_ref[...] = folded(context)


def route_kernel(layer, capacity, me_ref, core_ref, hidden_ref, *rest):
    parts, rest = rest[:4], rest[4:]
    pieces, rest = rest[:7], rest[7:]
    out_bias_ref, gain_ref, shift_ref, router_ref, ids_ref = rest[:5]
    middle_ref, second_ref, prob_ref, gate_ref, column_ref, send_ref, scratch, out_ref = rest[5:]
    count = len(parts)
    part_rows = pieces[1].shape[0]
    near = pl.multiple_of(core_ref[0] * part_rows, 16)
    away = pl.multiple_of((1 - core_ref[0]) * part_rows, 16)
    out_ref[0] = pieces[0][0]
    for step in range(1, count):
        out_ref[step, pl.ds(near, part_rows)] = pieces[step][...]
        out_ref[step, pl.ds(away, part_rows)] = pieces[count - 1 + step][...]
    for step in range(count):
        scratch[step] = parts[step][...]
    tokens = hidden_ref.shape[0]
    mix = None
    for j in range(count):
        turn = in_order(me_ref[0], j, count)
        context = unfolded(scratch[turn].astype(F32), tokens).astype(BF)
        part = dot(context, out_ref[turn])
        mix = part if mix is None else mix + part
    middle = hidden_ref[...].astype(F32) + mix + out_bias_ref[...].astype(F32)[layer : layer + 1]
    middle_ref[...] = middle
    unit, _ = normalized(middle)
    second_low = (unit * row_of(gain_ref, layer, 1) + row_of(shift_ref, layer, 1)).astype(BF)
    second_ref[...] = second_low
    prob = softmax_rows(dot_nt(second_low, router_ref[layer]))
    prob_ref[...] = prob
    ids = ids_ref[layer]
    experts = prob.shape[1]
    picks, columns = slot_columns(ids, experts, capacity)
    for k in range(2):
        gate_ref[:, k : k + 1] = jnp.sum(jnp.where(picks[k], prob, 0.0), axis=1, keepdims=True)
        column_ref[:, k : k + 1] = columns[k]
    slots = experts * capacity
    lookup = jnp.logical_or(one_hot(columns[0], slots), one_hot(columns[1], slots))
    width = second_low.shape[1]
    send_ref[:, :width] = dot_tn(low(lookup), second_low).astype(BF)
    if send_ref.shape[1] > width:
        lanes = lax.broadcasted_iota(jnp.int32, (tokens, send_ref.shape[1] - width), 1)
        total = None
        for k in range(2):
            rest_bits = jnp.sum(jnp.where(picks[k], prob, 0.0), axis=1, keepdims=True)
            wide = jnp.zeros(lanes.shape, F32)
            for piece in range(3):
                bits = rest_bits.astype(BF).astype(F32)
                wide = jnp.where(lanes == piece, bits, wide)
                rest_bits = rest_bits - bits
            part = dot_tn(low(one_hot(columns[k], slots)), wide.astype(BF))
            total = part if total is None else total + part
        send_ref[:, width:] = total.astype(BF)


def slot_columns(ids, experts, capacity):
    tokens = ids.shape[0]
    picks = [one_hot(ids[:, k : k + 1], experts) for k in range(2)]
    before = lax.broadcasted_iota(jnp.int32, (tokens, tokens), 0) > lax.broadcasted_iota(
        jnp.int32, (tokens, tokens), 1
    )
    earlier = dot(low(before), low(jnp.logical_or(picks[0], picks[1])))
    columns = []
    for k in range(2):
        slot = jnp.sum(jnp.where(picks[k], earlier, 0.0), axis=1, keepdims=True)
        columns.append(ids[:, k : k + 1] * capacity + slot.astype(jnp.int32))
    return picks, columns


def early_kernel(layer, capacity, experts, ids_ref, rows_ref, send_ref):
    _, columns = slot_columns(ids_ref[layer], experts, capacity)
    slots = experts * capacity
    lookup = jnp.logical_or(one_hot(columns[0], slots), one_hot(columns[1], slots))
    send_ref[...] = dot_tn(low(lookup), rows_ref[...]).astype(BF)


def send_kernel(joins, me_ref, base_ref, *rest):
    parts, rest = rest[:joins], rest[joins:]
    gate_ref, column_ref, send_ref = rest[:3]
    incoming = base_ref[...].astype(F32)
    if joins:
        incoming_out, scratch = rest[3:]
        rows = parts[0].shape[0]
        for step in range(joins):
            start = pl.multiple_of(in_order(me_ref[0], step, joins) * rows, 8)
            scratch[pl.ds(start, rows)] = parts[step][...].astype(F32)
        incoming = incoming + scratch[0 : incoming.shape[0]]
        incoming_out[...] = incoming
    slots = send_ref.shape[0]
    total = None
    for k in range(2):
        scaled = (gate_ref[:, k : k + 1] * incoming).astype(BF)
        part = dot_tn(low(one_hot(column_ref[:, k : k + 1], slots)), scaled)
        total = part if total is None else total + part
    send_ref[...] = total.astype(BF)


def combine_kernel(has_out, has_back, capacity, me_ref, arrived_ref, gate_ref, column_ref, *rest):
    devices, shards, half, _ = arrived_ref.shape
    rest = list(rest)
    incoming_ref = rest.pop(0) if has_back else None
    kept_ref = rest.pop(0) if not has_out else None
    share = 2 * (arrived_ref.shape[3] // (2 if has_out and has_back else 1)) // 4
    tile = 2 * share // 3
    rows = devices * half
    columns = [column_ref[:, k : k + 1] for k in range(2)]
    upper = [lax.rem(column, capacity) >= half for column in columns]
    fetch = [
        low(one_hot(lax.div(column, capacity) * half + lax.rem(column, half), rows))
        for column in columns
    ]

    def taken(first):
        lanes = slice(first, first + 2 * share)
        total = arrived_ref[:, 0, :, lanes].astype(F32)
        for j in range(1, shards):
            total = total + arrived_ref[:, j, :, lanes].astype(F32)
        table = total.reshape(rows, 2 * share).astype(BF)
        chosen = []
        for k in range(2):
            found = dot(fetch[k], table)
            mixed = found[:, 2 * tile :]
            lower = jnp.concatenate([found[:, :tile], mixed[:, : tile // 2]], axis=1)
            higher = jnp.concatenate([found[:, tile : 2 * tile], mixed[:, tile // 2 :]], axis=1)
            chosen.append(jnp.where(upper[k], higher, lower))
        return chosen

    if has_out:
        mixed_ref = rest.pop(0)
        chosen = taken(0)
        mixed_ref[...] = folded(gate_ref[:, 0:1] * chosen[0] + gate_ref[:, 1:2] * chosen[1])
        if not has_back:
            kept_out = rest.pop(0)
            for k in range(2):
                kept_out[k] = chosen[k].astype(BF)
    else:
        chosen = [kept_ref[k].astype(F32) for k in range(2)]
    if has_back:
        back_ref = rest.pop(0)
        found = taken(2 * share if has_out else 0)
        me = me_ref[0]
        first = incoming_ref[:, pl.ds(pl.multiple_of(me * tile, tile), tile)]
        start = pl.multiple_of((shards + lax.div(me, 2)) * tile, tile)
        last = incoming_ref[:, pl.ds(start, tile)]
        last = jnp.where(lax.rem(me, 2) == 0, last[:, : tile // 2], last[:, tile // 2 :])
        own = jnp.concatenate([first, last], axis=1).astype(F32)
        tokens = own.shape[0]
        lanes = lax.broadcasted_iota(jnp.int32, (2 * share, 128), 1)
        wide = jnp.zeros((2 * share, 128), F32)
        for k in range(2):
            gate_grad = jnp.sum(own * chosen[k], axis=1, keepdims=True)
            gate_grad = jnp.concatenate(
                [gate_grad, jnp.zeros((2 * share - tokens, 1), F32)], axis=0
            )
            upper_bits = gate_grad.astype(BF).astype(F32)
            wide = jnp.where(lanes == k, upper_bits, wide)
            wide = jnp.where(lanes == 2 + k, gate_grad - upper_bits, wide)
        back_ref[...] = folded(found[0] + found[1], wide.T[0:8])


def backward_block_kernel(layer, share, block, me_ref, incoming_ref, *rest):
    parts, rest = rest[:4], rest[4:]
    middle_ref, hidden_ref, prob_ref, gate_ref, ids_ref, qkv_ref = rest[:6]
    gain_ref, router_ref, out_weight_ref, weight_ref = rest[6:10]
    dh_ref, dqkv_ref, dz_ref, dlogit_ref, rows_ref = rest[10:15]
    block_refs = rest[15:19]
    unit_ref, inverse_ref, scratch, padded = rest[19:]
    me = me_ref[0]
    count = len(parts)
    for step in range(count):
        scratch[step] = parts[step][...]
    tokens = incoming_ref.shape[0]
    second_grad = joined_columns(scratch, me, count, tokens)
    gates = None
    for j in range(count):
        tail = scratch[in_order(me, j, count)].astype(F32)
        tail = tail[tail.shape[0] - 8 :]
        gates = tail if gates is None else gates + tail
    gates = jnp.concatenate([gates, jnp.zeros((120, gates.shape[1]), F32)], axis=0).T
    gates = (gates[:, 0:2] + gates[:, 2:4])[:tokens]
    prob = prob_ref[...]
    ids = ids_ref[layer]
    scaled = gates * gate_ref[...]
    prob_grad = jnp.zeros_like(prob)
    for k in range(2):
        prob_grad = prob_grad + jnp.where(
            one_hot(ids[:, k : k + 1], prob.shape[1]), gates[:, k : k + 1], 0.0
        )
    dlogit = (prob * (prob_grad - (scaled[:, 0:1] + scaled[:, 1:2]))).astype(BF)
    dlogit_ref[...] = dlogit
    second_grad = second_grad + dot(dlogit, router_ref[layer])
    unit_two, inverse_two = normalized(middle_ref[...])
    dh = incoming_ref[...].astype(F32) + norm_backward(
        second_grad, unit_two, inverse_two, row_of(gain_ref, layer, 1)
    )
    dh_ref[...] = dh
    dz = dh.astype(BF)
    dz_ref[...] = dz
    context_grad = dot_nt(dz, out_weight_ref[0]).astype(BF)
    queries, keys_low, values_low = qkv_ref[0], qkv_ref[1], qkv_ref[2]
    scale = HEAD ** (-0.5)
    grads = [[], [], []]
    for head in range(queries.shape[1] // HEAD):
        lanes = slice(head * HEAD, (head + 1) * HEAD)
        query, key, value = queries[:, lanes], keys_low[:, lanes], values_low[:, lanes]
        outer = context_grad[:, lanes]
        weights = softmax_rows(dot_nt(query, key) * scale)
        prob_dot = dot_nt(outer, value)
        score_grad = (
            weights * (prob_dot - jnp.sum(weights * prob_dot, axis=1, keepdims=True))
        ).astype(BF)
        grads[0].append(dot(score_grad, key) * scale)
        grads[1].append(dot_tn(score_grad, query) * scale)
        grads[2].append(dot_tn(weights.astype(BF), outer))
    partial = None
    sums = []
    for i in range(3):
        grad = jnp.concatenate(grads[i], axis=1).astype(BF)
        dqkv_ref[i] = grad
        sums.append(jnp.sum(grad.astype(F32), axis=0, keepdims=True))
        part = dot(grad, weight_ref[0, i])
        partial = part if partial is None else partial + part
    unit_one, inverse_one = normalized(hidden_ref[...].astype(F32))
    width = partial.shape[1]
    rows_ref[...] = jnp.zeros_like(rows_ref)
    rows_ref[0:1] = jnp.sum(second_grad * unit_two, axis=0, keepdims=True)
    rows_ref[1:2] = jnp.sum(second_grad, axis=0, keepdims=True)
    rows_ref[2:3] = jnp.sum(dh, axis=0, keepdims=True)
    rows_ref[3:4] = jnp.concatenate(
        [sums[0], sums[2], jnp.zeros((1, width - 2 * share), F32)], axis=1
    )
    rows_ref[4:5] = jnp.sum(partial * unit_one, axis=0, keepdims=True)
    rows_ref[5:6] = jnp.sum(partial, axis=0, keepdims=True)

    def spread_rows(values):
        padded[...] = jnp.zeros_like(padded)
        padded[0:tokens] = values

    def rows_of(step):
        start = pl.multiple_of(lax.rem(me + step, count) * block, 8)
        return padded[pl.ds(start, block)]

    spread_rows(partial)
    for step in range(count):
        block_refs[step][...] = rows_of(step).astype(BF)
    spread_rows(unit_one)
    unit_ref[...] = rows_of(0)
    spread_rows(jnp.broadcast_to(inverse_one, partial.shape))
    inverse_ref[...] = rows_of(0)[:, 0:128]


def norm_rows_kernel(layer, p0, p1, p2, p3, unit_ref, inverse_ref, gain_ref, out_ref):
    total = p0[...].astype(F32) + p1[...].astype(F32) + p2[...].astype(F32) + p3[...].astype(F32)
    out_ref[...] = norm_backward(
        total, unit_ref[...], inverse_ref[:, 0:1], row_of(gain_ref, layer, 0)
    ).astype(BF)


def pack_kernel(first_ref, dqkv_ref, context_ref, dz_ref, second_ref, dlogit_ref, rows_ref, core_ref, mine_ref, away_ref, target):
    width = first_ref.shape[1]
    share = dqkv_ref.shape[2]
    experts = dlogit_ref.shape[1]
    half = (width + experts) // 2
    size = target.shape[0] // 2
    gap = size - half

    def put(start, values):
        stop = start + values.shape[0]
        if stop <= half:
            target[start:stop] = values
        elif start >= half:
            target[start + gap : stop + gap] = values
        else:
            target[start:half] = values[: half - start]
            target[size : stop + gap] = values[half - start :]

    first_low = first_ref[...]
    for i in range(3):
        put(i * share, dot_tn(dqkv_ref[i], first_low))
    put(3 * share, dot_tn(context_ref[...], dz_ref[...]))
    put(width, dot_tn(dlogit_ref[...], second_ref[...]))
    small = jnp.concatenate([rows_ref[...], jnp.zeros((gap - 8, width), F32)], axis=0)
    target[half:size] = small
    target[size + half :] = small
    core = core_ref[0]
    mine_ref[...] = target[pl.ds(pl.multiple_of(core * size, 8), size)].astype(BF)
    away_ref[...] = target[pl.ds(pl.multiple_of((1 - core) * size, 8), size)].astype(BF)


def sum_kernel(count, pieces, index_ref, *rest):
    parts, outs, scratch = rest[:count], rest[count : count + pieces], rest[-1]
    total = parts[0][...].astype(F32)
    for part in parts[1:]:
        total = total + part[...].astype(F32)
    if pieces == 1:
        outs[0][...] = total.astype(BF)
        return
    rows = outs[0].shape[0]
    scratch[0 : total.shape[0]] = total
    if scratch.shape[0] > total.shape[0]:
        scratch[total.shape[0] :] = jnp.zeros(
            (scratch.shape[0] - total.shape[0], total.shape[1]), F32
        )
    for step in range(pieces):
        start = pl.multiple_of(lax.rem(index_ref[0] + step, pieces) * rows, 8)
        outs[step][...] = scratch[pl.ds(start, rows)].astype(BF)


def ordered_sum_kernel(count, index_ref, *rest):
    parts, out_ref, scratch = rest[:count], rest[count], rest[count + 1]
    for step in range(count):
        scratch[step] = parts[step][...].astype(F32)
    total = scratch[in_order(index_ref[0], 0, count)]
    for j in range(1, count):
        total = total + scratch[in_order(index_ref[0], j, count)]
    out_ref[...] = total.astype(BF)


def order_kernel(count, index_ref, *rest):
    parts, out_ref, scratch = rest[:count], rest[count], rest[count + 1]
    rows = parts[0].shape[0]
    for step in range(count):
        start = pl.multiple_of(in_order(index_ref[0], step, count) * rows, 8)
        scratch[pl.ds(start, rows)] = parts[step][...].astype(F32)
    out_ref[...] = scratch[0 : out_ref.shape[0]].astype(BF)


def add_rows_kernel(count, me_ref, base_ref, *rest):
    parts, out_ref, scratch = rest[:count], rest[count], rest[count + 1]
    rows = parts[0].shape[0]
    for step in range(count):
        start = pl.multiple_of(in_order(me_ref[0], step, count) * rows, 8)
        scratch[pl.ds(start, rows)] = parts[step][...].astype(F32)
    out_ref[...] = base_ref[...] + scratch[0 : out_ref.shape[0]]


def add_columns_kernel(count, me_ref, base_ref, *rest):
    parts, out_ref, scratch = rest[:count], rest[count], rest[count + 1]
    for step in range(count):
        scratch[step] = parts[step][...]
    out_ref[...] = base_ref[...] + joined_columns(scratch, me_ref[0], count, out_ref.shape[0])


def unpack_kernel(core_ref, me_ref, *rest):
    levels, smalls, outs = rest[:4], rest[4:8], rest[8:15]
    scratch, small_scratch = rest[15:]
    inw_ref, outw_ref, route_ref, gain_ref, shift_ref, inb_ref, outb_ref = outs
    size = levels[0].shape[0]
    core = core_ref[0]
    share, width = inw_ref.shape[2], inw_ref.shape[3]
    experts = route_ref.shape[1]
    half = (width + experts) // 2
    gap = size - half
    count = len(smalls)
    for step in range(count):
        small_scratch[step] = smalls[step][...].astype(F32)
    small = small_scratch[in_order(me_ref[0], 0, count)]
    for j in range(1, count):
        small = small + small_scratch[in_order(me_ref[0], j, count)]
    for layer in range(2):
        mine_ref, other_ref = levels[2 * layer], levels[2 * layer + 1]
        scratch[pl.ds(pl.multiple_of(core * size, 8), size)] = mine_ref[...].astype(F32)
        scratch[pl.ds(pl.multiple_of((1 - core) * size, 8), size)] = other_ref[...].astype(F32)

        def rows(start, stop):
            if stop <= half:
                return scratch[start:stop]
            if start >= half:
                return scratch[start + gap : stop + gap]
            return jnp.concatenate([scratch[start:half], scratch[size : stop + gap]], axis=0)

        for i in range(3):
            inw_ref[layer, i] = rows(i * share, (i + 1) * share)
        outw_ref[layer] = rows(3 * share, width)
        route_ref[layer] = rows(width, width + experts)
        firsts = small[8 * layer + 4 : 8 * layer + 6]
        seconds = scratch[half : half + 4]
        gain_ref[layer, 0:1] = firsts[0:1]
        gain_ref[layer, 1:2] = seconds[0:1]
        shift_ref[layer, 0:1] = firsts[1:2]
        shift_ref[layer, 1:2] = seconds[1:2]
        outb_ref[layer : layer + 1] = seconds[2:3]
        inb_ref[layer, 0:1] = seconds[3:4, :share]
        inb_ref[layer, 1:2] = seconds[3:4, share : 2 * share]


def write_chunks(total, out_ref, part_index=0):
    devices, _, half, _ = out_ref.shape
    rows = total.reshape(devices, 2 * half, total.shape[1])
    lower, upper = rows[:, :half], rows[:, half:]
    tile = total.shape[1] // 6
    part = tile // 2
    for j in range(4):
        first = slice(j * tile, (j + 1) * tile)
        rest = slice(4 * tile + j * part, 4 * tile + (j + 1) * part)
        mixed = jnp.concatenate([lower[:, :, rest], upper[:, :, rest]], axis=2)
        block = jnp.concatenate([lower[:, :, first], upper[:, :, first], mixed], axis=2)
        lanes = slice(part_index * 3 * tile, (part_index + 1) * 3 * tile)
        out_ref[:, j, :, lanes] = block.astype(BF)


def forward_kernel(layer, me_ref, x_ref, up_ref, up_bias_ref, down_ref, down_bias_ref, chunk_ref, active_ref, slope_ref, total):
    step = pl.program_id(0)
    rows = x_ref[...].reshape(total.shape)
    pre = jnp.dot(rows, up_ref[0, 0], preferred_element_type=F32)
    pre = pre + up_bias_ref[...].astype(F32)[0, layer : layer + 1]
    half_cdf = 0.5 * (1.0 + lax.erf(pre * 0.7071067811865476))
    active = (pre * half_cdf).astype(BF)
    active_ref[...] = active
    slope_ref[...] = half_cdf + pre * jnp.exp(-0.5 * pre * pre) * 0.3989422804014327
    part = jnp.dot(active, down_ref[0, 0], preferred_element_type=F32)

    @pl.when(step == 0)
    def _():
        offset = down_bias_ref[...].astype(F32)[0, layer : layer + 1]
        total[...] = part + jnp.where(me_ref[0] == 0, offset, 0.0)

    @pl.when(step > 0)
    def _():
        total[...] += part

    @pl.when(step == pl.num_programs(0) - 1)
    def _():
        write_chunks(total[...], chunk_ref)


def backward_kernel(dy_ref, slope_ref, up_ref, down_ref, chunk_ref, pre_grad_ref, total):
    step = pl.program_id(0)
    out_grad = dy_ref[...].reshape(total.shape)
    pre_grad = (dot_nt(out_grad, down_ref[0, 0]) * slope_ref[...]).astype(BF)
    pre_grad_ref[...] = pre_grad
    part = dot_nt(pre_grad, up_ref[0, 0])

    @pl.when(step == 0)
    def _():
        total[...] = part

    @pl.when(step > 0)
    def _():
        total[...] += part

    @pl.when(step == pl.num_programs(0) - 1)
    def _():
        write_chunks(total[...], chunk_ref)


def both_kernel(
    layer,
    me_ref,
    x_ref,
    grad_ref,
    up_ref,
    up_bias_ref,
    down_ref,
    down_bias_ref,
    chunk_ref,
    active_ref,
    pre_grad_ref,
    dy_ref,
    out_total,
    back_total,
):
    step = pl.program_id(0)
    rows, width = out_total.shape

    @pl.when(step == 0)
    def _():
        gate = jnp.sum(x_ref[:, :, width:].astype(F32).reshape(rows, -1), axis=1, keepdims=True)
        dy_ref[...] = (gate * grad_ref[...].reshape(rows, width).astype(F32)).astype(BF).reshape(
            dy_ref.shape
        )
        offset = down_bias_ref[...].astype(F32)[0, layer : layer + 1]
        offset = jnp.where(me_ref[0] == 0, offset, 0.0)
        out_total[...] = jnp.broadcast_to(offset, out_total.shape)
        back_total[...] = jnp.zeros_like(back_total)

    arrived = x_ref[:, :, :width].reshape(rows, width)
    pre = dot(arrived, up_ref[0, 0]) + up_bias_ref[...].astype(F32)[0, layer : layer + 1]
    half_cdf = 0.5 * (1.0 + lax.erf(pre * 0.7071067811865476))
    active = (pre * half_cdf).astype(BF)
    active_ref[...] = active
    slope = half_cdf + pre * jnp.exp(-0.5 * pre * pre) * 0.3989422804014327
    out_total[...] += dot(active, down_ref[0, 0])
    pre_grad = (dot_nt(dy_ref[...].reshape(rows, width), down_ref[0, 0]) * slope).astype(BF)
    pre_grad_ref[...] = pre_grad
    back_total[...] += dot_nt(pre_grad, up_ref[0, 0])

    @pl.when(step == pl.num_programs(0) - 1)
    def _():
        write_chunks(out_total[...], chunk_ref, 0)
        write_chunks(back_total[...], chunk_ref, 1)


def weight_kernel(x_ref, dy_ref, active_ref, pre_grad_ref, *rest):
    up_ref, up_bias_ref, down_ref, down_bias_ref = rest[-4:]
    shape = active_ref.shape[0], dy_ref.shape[2]
    pre_grad = pre_grad_ref[...]
    out_grad = dy_ref[...].reshape(shape)
    up_ref[0, 0] = dot_tn(x_ref[...].reshape(shape), pre_grad)
    down_ref[0, 0] = dot_tn(active_ref[...], out_grad)
    up_bias_ref[0] = jnp.sum(pre_grad.astype(F32), axis=0, keepdims=True)

    @pl.when(pl.program_id(0) == 0)
    def _():
        down_bias_ref[0] = jnp.sum(out_grad.astype(F32), axis=0, keepdims=True)


FBLOCK = 768
BOTH_BLOCK = 384
PARAMS = dict(vmem_limit_bytes=48 * 1024 * 1024)


def smem():
    return pl.BlockSpec(memory_space=pltpu.SMEM)


def near_out(shape, kind):
    return jax.ShapeDtypeStruct(shape, kind)


def far_out(shape, kind):
    return pltpu.HBM(shape, kind)


def far(value):
    return pltpu.with_memory_space_constraint(value, pltpu.HBM)


def call(kernel, name, outs, operands, scratch=(), specs=None):
    specs = specs or {}
    in_specs = [
        specs.get(i, smem() if operand.shape == (1,) else whole(operand.shape))
        for i, operand in enumerate(operands)
    ]
    return pl.pallas_call(
        kernel,
        grid=(1,),
        in_specs=in_specs,
        out_specs=[whole(out.shape) for out in outs],
        out_shape=outs,
        scratch_shapes=[pltpu.VMEM(shape, kind) for shape, kind in scratch],
        compiler_params=pltpu.CompilerParams(**PARAMS),
        name=name,
    )(*operands)


def layer_block(array, layer):
    shape = (1,) + array.shape[1:]
    return pl.BlockSpec(shape, lambda step: (layer,) + (0,) * (len(shape) - 1))


def whole(shape):
    return pl.BlockSpec(shape, lambda step: (0,) * len(shape))


def expert_forward(layer, me_one, arrived, up_weight, up_bias, down_weight, down_bias):
    devices, slots, width = arrived.shape
    hidden = up_weight.shape[3]
    rows = devices * slots
    return pl.pallas_call(
        functools.partial(forward_kernel, layer),
        grid=(hidden // FBLOCK,),
        in_specs=[
            smem(),
            whole(arrived.shape),
            pl.BlockSpec((1, 1, width, FBLOCK), lambda step: (layer, 0, 0, step)),
            pl.BlockSpec((1, up_bias.shape[1], FBLOCK), lambda step: (0, 0, step)),
            pl.BlockSpec((1, 1, FBLOCK, width), lambda step: (layer, 0, step, 0)),
            whole(down_bias.shape),
        ],
        out_specs=[
            whole((devices, 4, slots // 2, width // 2)),
            pl.BlockSpec((rows, FBLOCK), lambda step: (0, step)),
            pl.BlockSpec((rows, FBLOCK), lambda step: (0, step)),
        ],
        out_shape=[
            jax.ShapeDtypeStruct((devices, 4, slots // 2, width // 2), BF),
            pltpu.HBM((rows, hidden), BF),
            pltpu.HBM((rows, hidden), F32),
        ],
        scratch_shapes=[pltpu.VMEM((rows, width), F32)],
        compiler_params=pltpu.CompilerParams(**PARAMS),
        name="expert_forward",
    )(me_one, arrived, *map(far, (up_weight, up_bias, down_weight, down_bias)))


def expert_backward(layer, out_grad, slope, up_weight, down_weight):
    devices, slots, width = out_grad.shape
    hidden = up_weight.shape[3]
    rows = devices * slots
    chunk = (devices, 4, slots // 2, width // 2)
    return pl.pallas_call(
        backward_kernel,
        grid=(hidden // FBLOCK,),
        in_specs=[
            whole(out_grad.shape),
            pl.BlockSpec((rows, FBLOCK), lambda step: (0, step)),
            pl.BlockSpec((1, 1, width, FBLOCK), lambda step: (layer, 0, 0, step)),
            pl.BlockSpec((1, 1, FBLOCK, width), lambda step: (layer, 0, step, 0)),
        ],
        out_specs=[whole(chunk), pl.BlockSpec((rows, FBLOCK), lambda step: (0, step))],
        out_shape=[jax.ShapeDtypeStruct(chunk, BF), pltpu.HBM((rows, hidden), BF)],
        scratch_shapes=[pltpu.VMEM((rows, width), F32)],
        compiler_params=pltpu.CompilerParams(**PARAMS),
        name="expert_backward",
    )(out_grad, *map(far, (slope, up_weight, down_weight)))


def expert_both(layer, me_one, arrived, grad_rows, up_weight, up_bias, down_weight, down_bias):
    devices, slots, width = grad_rows.shape
    hidden = up_weight.shape[3]
    rows = devices * slots
    chunk = (devices, 4, slots // 2, width)
    return pl.pallas_call(
        functools.partial(both_kernel, layer),
        grid=(hidden // BOTH_BLOCK,),
        in_specs=[
            smem(),
            whole(arrived.shape),
            whole(grad_rows.shape),
            pl.BlockSpec((1, 1, width, BOTH_BLOCK), lambda step: (layer, 0, 0, step)),
            pl.BlockSpec((1, up_bias.shape[1], BOTH_BLOCK), lambda step: (0, 0, step)),
            pl.BlockSpec((1, 1, BOTH_BLOCK, width), lambda step: (layer, 0, step, 0)),
            whole(down_bias.shape),
        ],
        out_specs=[
            whole(chunk),
            pl.BlockSpec((rows, BOTH_BLOCK), lambda step: (0, step)),
            pl.BlockSpec((rows, BOTH_BLOCK), lambda step: (0, step)),
            whole(grad_rows.shape),
        ],
        out_shape=[
            jax.ShapeDtypeStruct(chunk, BF),
            pltpu.HBM((rows, hidden), BF),
            pltpu.HBM((rows, hidden), BF),
            pltpu.HBM(grad_rows.shape, BF),
        ],
        scratch_shapes=[pltpu.VMEM((rows, width), F32), pltpu.VMEM((rows, width), F32)],
        compiler_params=pltpu.CompilerParams(**PARAMS),
        name="expert_both",
    )(me_one, arrived, *map(far, (grad_rows, up_weight, up_bias, down_weight, down_bias)))


def expert_weights(layer, layers, arrived, out_grad, active, pre_grad, earlier):
    devices, slots, width = out_grad.shape
    rows, hidden = active.shape
    operands = [*map(far, (arrived, out_grad, active, pre_grad))] + list(earlier or ())
    return pl.pallas_call(
        weight_kernel,
        grid=(hidden // FBLOCK,),
        in_specs=[
            whole(out_grad.shape),
            whole(out_grad.shape),
            pl.BlockSpec((rows, FBLOCK), lambda step: (0, step)),
            pl.BlockSpec((rows, FBLOCK), lambda step: (0, step)),
        ]
        + [pl.BlockSpec(memory_space=pl.ANY)] * len(earlier or ()),
        out_specs=[
            pl.BlockSpec((1, 1, width, FBLOCK), lambda step: (layer, 0, 0, step)),
            pl.BlockSpec((1, 1, FBLOCK), lambda step: (layer, 0, step)),
            pl.BlockSpec((1, 1, FBLOCK, width), lambda step: (layer, 0, step, 0)),
            pl.BlockSpec((1, 1, width), lambda step: (layer, 0, 0)),
        ],
        out_shape=[
            pltpu.HBM((layers, 1, width, hidden), F32),
            pltpu.HBM((layers, 1, hidden), F32),
            pltpu.HBM((layers, 1, hidden, width), F32),
            pltpu.HBM((layers, 1, width), F32),
        ],
        input_output_aliases={4 + i: i for i in range(len(earlier or ()))},
        compiler_params=pltpu.CompilerParams(**PARAMS),
        name="expert_weights",
    )(*operands)


def cycle(size, step):
    return [(place, (place + step) % size) for place in range(size)]


def body(
    tokens,
    expert_ids,
    norm_gain,
    norm_bias,
    input_weight,
    input_bias,
    output_weight,
    output_bias,
    router_weight,
    up_weight,
    up_bias,
    down_weight,
    down_bias,
    cotangent,
):
    token_count, width = tokens.shape
    layer_count = norm_gain.shape[0]
    share = input_weight.shape[3]
    experts = router_weight.shape[2]
    devices = lax.axis_size("expert")
    shards = lax.axis_size("shard")
    capacity = 5 * token_count // (2 * experts) + 1
    slots = experts * capacity
    me = lax.axis_index("shard")
    place = lax.axis_index("expert")
    me_one = me.reshape(1)
    row_block = 8 * (-(-token_count // (8 * shards)))
    size = 32 * (-(-((width + experts) // 2 + 8) // 32))

    cores = 2
    side = 4
    core, z_place, x_place = place % cores, (place // cores) % side, place // (cores * side)
    core_one, z_one, x_one = core.reshape(1), z_place.reshape(1), x_place.reshape(1)

    def core_pairs():
        return [(p, p ^ 1) for p in range(devices)]

    def z_pairs(step):
        return [(p, (p // 8) * 8 + ((p // 2 + step) % 4) * 2 + p % 2) for p in range(devices)]

    def x_pairs(step):
        return [(p, ((p // 8 + step) % 4) * 8 + p % 8) for p in range(devices)]

    def spread(value):
        return [value] + [
            lax.ppermute(value, "shard", cycle(shards, step)) for step in range(1, shards)
        ]

    def exchange(blocks):
        return [blocks[0]] + [
            lax.ppermute(blocks[step], "shard", cycle(shards, step)) for step in range(1, shards)
        ]

    def to_owners(rows):
        outgoing = rows.reshape(devices, capacity, rows.shape[1])
        return lax.all_to_all(outgoing, "expert", split_axis=0, concat_axis=0, tiled=True)

    def go_back(chunks):
        flat = chunks.reshape(-1, *chunks.shape[2:])
        back = lax.all_to_all(
            flat, ("expert", "shard"), split_axis=0, concat_axis=0, tiled=True
        )
        return back.reshape(chunks.shape)

    gains, shifts = far(norm_gain), far(norm_bias)
    in_bias, out_bias = far(input_bias), far(output_bias)
    up_rows, down_rows = jnp.swapaxes(up_bias, 0, 1), jnp.swapaxes(down_bias, 0, 1)
    ids = far(expert_ids)
    pair = (token_count, 2)
    square = (token_count, width)
    narrow = (token_count, share)
    fold_rows = 8 * (-(-token_count // 16))
    fold = (fold_rows, 2 * share)
    fold_more = (fold_rows + 8, 2 * share)
    in_weight = far(jnp.swapaxes(input_weight, 2, 3))
    router = far(jnp.swapaxes(router_weight, 1, 2))
    out_weight = far(output_weight)

    def attention_forward(layer, base, parts):
        joins = len(parts)
        operands = [me_one, base, *parts, gains, shifts, in_weight, in_bias]
        outs = [
            far_out(square, BF),
            far_out((3,) + narrow, BF),
            far_out(narrow, BF),
            near_out(fold, BF),
        ]
        scratch = []
        if joins:
            outs.append(far_out(square, F32))
            scratch.append(((joins,) + fold, BF))
        found = call(
            functools.partial(attention_kernel, layer, joins),
            "attention_forward",
            outs,
            operands,
            scratch,
            specs={joins + 4: layer_block(in_weight, layer)},
        )
        return found if joins else [*found, base]

    def weight_pieces(weight):
        rows = weight.shape[0] // cores
        near = spread(lax.dynamic_slice_in_dim(weight, core * rows, rows, 0))[1:]
        return near + [to_core(value) for value in near]

    def route(layer, hidden, context_fold, pieces, more=0):
        return call(
            functools.partial(route_kernel, layer, capacity),
            "route",
            [
                far_out(square, F32),
                far_out(square, BF),
                far_out((token_count, experts), F32),
                far_out(pair, F32),
                far_out(pair, jnp.int32),
                near_out((slots, width + more), BF),
            ],
            [
                me_one,
                core_one,
                far(hidden),
                *context_fold,
                out_weight,
                *pieces,
                out_bias,
                gains,
                shifts,
                router,
                ids,
            ],
            [((shards,) + fold, BF), ((shards, share, width), BF)],
            specs={7: layer_block(out_weight, layer)},
        )

    def send_grads(base, parts, gate_values, columns):
        joins = len(parts)
        outs = [near_out((slots, width), BF)]
        scratch = []
        if joins:
            outs.append(far_out(square, F32))
            scratch.append(((joins * row_block, width), F32))
        return call(
            functools.partial(send_kernel, joins),
            "send_grads",
            outs,
            [me_one, base, *parts, far(gate_values), far(columns)],
            scratch,
        )

    def combine(arrived, gate_values, columns, incoming=None, kept=None):
        has_back, has_out = incoming is not None, kept is None
        outs = []
        if has_out:
            outs.append((far_out if has_back else near_out)(fold, BF))
            if not has_back:
                outs.append(far_out((2,) + narrow, BF))
        if has_back:
            outs.append(near_out(fold_more, BF))
        operands = [me_one, arrived, far(gate_values), far(columns)]
        operands += [far(value) for value in (incoming, kept) if value is not None]
        return call(
            functools.partial(combine_kernel, has_out, has_back, capacity),
            "combine",
            outs,
            operands,
        )

    def run_forward(layer, arrived):
        return expert_forward(layer, me_one, arrived, up_weight, up_rows, down_weight, down_rows)

    def block_backward(layer, incoming, parts, middle, hidden, prob, gate_values, qkv):
        block = near_out((row_block, width), BF)
        out = near_out if layer == 0 else far_out
        return call(
            functools.partial(backward_block_kernel, layer, share, row_block),
            "backward_block",
            [
                (far_out if layer == 0 else near_out)(square, F32),
                out((3,) + narrow, BF),
                out(square, BF),
                out((token_count, experts), BF),
                out((8, width), F32),
                block,
                block,
                block,
                block,
                near_out((row_block, width), F32),
                near_out((row_block, 128), F32),
            ],
            [
                me_one,
                far(incoming),
                *parts,
                far(middle),
                far(hidden),
                far(prob),
                far(gate_values),
                ids,
                far(qkv),
                gains,
                router,
                out_weight,
                in_weight,
            ],
            [((shards,) + fold_more, BF), ((shards * row_block, width), F32)],
            specs={
                14: layer_block(output_weight, layer),
                15: layer_block(in_weight, layer),
            },
        )

    def norm_rows(layer, blocks, unit, inverse):
        return call(
            functools.partial(norm_rows_kernel, layer),
            "norm_rows",
            [near_out((row_block, width), BF)],
            [*blocks, unit, inverse, gains],
        )[0]

    def pack(first_low, dqkv, context, dz, second_low, dlogit, rows):
        half = near_out((size, width), BF)
        return call(
            pack_kernel,
            "pack",
            [half, half],
            [first_low, dqkv, context, dz, second_low, dlogit, rows, core_one],
            [((2 * size, width), F32)],
        )

    quarter = size // side

    def sums(parts, index, pieces, rows):
        return call(
            functools.partial(sum_kernel, len(parts), pieces),
            "sums",
            [near_out((rows, width), BF)] * pieces,
            [index, *parts],
            [((pieces * rows, width), F32)],
        )

    def ordered_sum(parts, index):
        shape = parts[0].shape
        return call(
            functools.partial(ordered_sum_kernel, len(parts)),
            "ordered_sum",
            [near_out(shape, BF)],
            [index, *parts],
            [((len(parts),) + shape, F32)],
        )[0]

    def ordered(parts, index, rows):
        return call(
            functools.partial(order_kernel, len(parts)),
            "ordered",
            [near_out((rows, width), BF)],
            [index, *parts],
            [((len(parts) * parts[0].shape[0], width), F32)],
        )[0]

    def sent(blocks, pairs):
        return [blocks[0]] + [
            lax.ppermute(blocks[step], "expert", pairs(step)) for step in range(1, side)
        ]

    def to_core(value):
        return lax.ppermute(value, "expert", core_pairs())

    def tied(*values):
        return lax.optimization_barrier(values)

    pieces = weight_pieces(output_weight[0])
    first0, qkv0, context0, fold0, hidden0 = attention_forward(0, tokens, [])
    middle0, second0, prob0, gate0, column0, send = route(0, hidden0, spread(fold0), pieces)
    send, later_weight = tied(send, output_weight[1])
    arrived0 = to_owners(send)
    arrived0, *pieces = tied(arrived0, *weight_pieces(later_weight))
    chunks, active0, slope0 = run_forward(0, arrived0)
    back = go_back(chunks)
    mixed, kept0 = combine(back, gate0, column0)

    mixed_parts = spread(mixed)
    (send_rows,) = call(
        functools.partial(early_kernel, 1, capacity, experts),
        "early_rows",
        [far_out((slots, width), BF)],
        [ids, far(cotangent)],
    )
    send_rows, mixed_parts[0] = tied(send_rows, mixed_parts[0])
    first1, qkv1, context1, fold1, hidden1 = attention_forward(1, far(middle0), mixed_parts)
    grad_rows = to_owners(send_rows)
    grad_rows, *fold1 = tied(grad_rows, *spread(fold1))
    middle1, second1, prob1, gate1, column1, send = route(1, hidden1, fold1, pieces, 128)
    arrived1 = to_owners(send)
    chunks, active1, pre_grad1, out_grad1 = expert_both(
        1, me_one, arrived1, grad_rows, up_weight, up_rows, down_weight, down_rows
    )
    back = go_back(chunks)
    expert_grads = expert_weights(
        1, layer_count, arrived1, out_grad1, active1, pre_grad1, None
    )
    back, *expert_grads = tied(back, *expert_grads)
    mixed, shares = combine(back, gate1, column1, incoming=cotangent)

    dh1, dqkv1, dz1, dlogit1, rows1, *blocks, unit, inverse = block_backward(
        1, cotangent, spread(shares), middle1, hidden1, prob1, gate1, qkv1
    )
    parts = spread(norm_rows(1, exchange(blocks), unit, inverse))
    send, incoming = send_grads(dh1, parts, gate0, column0)

    out_grad0 = to_owners(send)
    mine1, away1 = pack(*map(far, (first1, dqkv1, context1, dz1, second1, dlogit1, rows1)))
    away1 = to_core(away1)
    level1 = sent(sums([mine1, away1], x_one, side, quarter), x_pairs)
    mixed = spread(mixed)
    output = call(
        functools.partial(add_columns_kernel, shards),
        "add_columns",
        [far_out(square, F32)],
        [me_one, far(middle1), *mixed],
        [((shards,) + fold, BF)],
    )[0]
    out_grad0, output, *level1 = tied(out_grad0, output, *level1)
    back_chunks, pre_grad0 = expert_backward(0, out_grad0, slope0, up_weight, down_weight)
    back = go_back(back_chunks)
    expert_grads = expert_weights(
        0, layer_count, arrived0, out_grad0, active0, pre_grad0, expert_grads
    )
    level1 = sent(sums(level1, x_one, 1, quarter) * side, z_pairs)
    back, *level1 = tied(back, *level1)
    (shares,) = combine(back, gate0, column0, incoming=incoming, kept=kept0)
    shares = spread(shares)
    dh0, dqkv0, dz0, dlogit0, rows0, *blocks, unit, inverse = block_backward(
        0, incoming, shares, middle0, hidden0, prob0, gate0, qkv0
    )
    level1 = sent([ordered_sum(level1, z_one)] * side, x_pairs)
    dqkv0, *level1 = tied(dqkv0, *level1)
    mine, away = pack(
        far(first0), dqkv0, far(context0), dz0, far(second0), dlogit0, rows0
    )
    away = to_core(away)

    level1 = ordered(level1, x_one, size)
    other1 = to_core(level1)
    away, other1 = tied(away, other1)
    blocks = exchange(blocks)
    level = sent(sums([mine, away], z_one, side, quarter), z_pairs)
    rest = tied(*level, *blocks)
    level, blocks = rest[:side], rest[side:]
    level = sent(sums(level, z_one, 1, quarter) * side, x_pairs)
    parts = spread(norm_rows(0, blocks, unit, inverse))
    rest = tied(*level, *parts)
    level, parts = rest[:side], rest[side:]
    level = sent([ordered_sum(level, x_one)] * side, z_pairs)
    rest = tied(*level, *expert_grads)
    level, expert_grads = rest[:side], rest[side:]
    level = ordered(level, z_one, size)
    other = to_core(level)
    half = (width + experts) // 2
    small = spread(jnp.concatenate([level[half : half + 8], level1[half : half + 8]], axis=0))
    grad_tokens = call(
        functools.partial(add_rows_kernel, shards),
        "add_rows",
        [far_out(square, F32)],
        [me_one, far(dh0), *parts],
        [((shards * row_block, width), F32)],
    )[0]
    inw, outw, router_grad, gain_grad, shift_grad, inb, outb = call(
        unpack_kernel,
        "unpack",
        [
            far_out((layer_count, 3, share, width), F32),
            far_out((layer_count, share, width), F32),
            far_out((layer_count, experts, width), F32),
            far_out((layer_count, 2, width), F32),
            far_out((layer_count, 2, width), F32),
            far_out((layer_count, 2, share), F32),
            far_out((layer_count, width), F32),
        ],
        [core_one, me_one, level, other, level1, other1, *small],
        [((2 * size, width), F32), ((shards, 16, width), F32)],
    )
    return (
        output,
        grad_tokens,
        gain_grad,
        shift_grad,
        jnp.swapaxes(inw, 2, 3),
        inb,
        outw,
        outb,
        jnp.swapaxes(router_grad, 1, 2),
        *expert_grads,
    )


def solution(mesh):
    return jax.shard_map(
        body,
        mesh=mesh,
        in_specs=(
            P("expert", None),
            P(None, "expert", None),
            P(),
            P(),
            P(None, None, None, "shard"),
            P(None, None, "shard"),
            P(None, "shard", None),
            P(),
            P(),
            P(None, "expert", None, "shard"),
            P(None, "expert", "shard"),
            P(None, "expert", "shard", None),
            P(None, "expert", None),
            P("expert", None),
        ),
        out_specs=(
            P("expert", None),
            P("expert", None),
            P(),
            P(),
            P(None, None, None, "shard"),
            P(None, None, "shard"),
            P(None, "shard", None),
            P(),
            P(),
            P(None, "expert", None, "shard"),
            P(None, "expert", "shard"),
            P(None, "expert", "shard", None),
            P(None, "expert", None),
        ),
        check_vma=False,
    )
```
